512 devices in a mesh: chan: 32 (over x_lo, y, core), inp: 16 (over x_hi, z).
Axes of the slice: x: 4 (x_hi: 2, x_lo: 2; x = x_hi * 2 + x_lo), y: 8, z: 8, core: 2. Of those that a mesh axis runs over, the one named last changes fastest.
Arguments:
- volts: bfloat16 [2, 1024, 32, 14336], P(None, ('inp', 'chan')), may hold values from -6 to 6
- pfb_taps: float32 [6, 2048], replicated, may hold values from -2.5 to 2.5
- channel_order: int32 [32], replicated, may hold values from 0 to 31, each once
- station_slot: int32 [512], replicated, may hold values from 0 to 511, each once
Outputs:
- visibilities: float32 [32, 2, 2, 1024, 1024], P('chan', None, None, 'inp')
The draws below stay inside these ranges and needn't reach their ends.
Inputs may be any that keep to these rules, and one draw needn't show every extreme that they name: `channel_order`: each coarse channel appears once. `station_slot`: each input pair carries one station.
All inputs are finite; a program needn't handle non-finite values.
Results may differ from the reference program's by a relative error of at most 0.0053.
Values may be sent and summed in bfloat16 or wider, within the bound.
A program may use at most 64 MiB of HBM per device.

```python
import math
import jax
import jax.numpy as jnp
from jax import lax

STATIONS = 512
FINE = 2048
FA = 64
TAPS = 6
FGROUP = 1024
INPUTS = 1024
OUTCH = 2
SAMPLES = 14336
CHANNELS = 32


def block_levels(key, extent, shards, smallest, top_value):
    factor_of, own = 1.0, jax.random.fold_in(key, 6)
    for dim, blocks in shards:
        steps = jnp.exp(jax.random.uniform(jax.random.fold_in(own, dim), (blocks,), jnp.float32, smallest / len(shards), top_value / len(shards)))
        factor_of = factor_of * jnp.repeat(steps, extent[dim] // blocks).reshape([-1 if axis == dim else 1 for axis in range(len(extent))])
    return factor_of


def gaussian(stream_key, extent, deviation, most, shards=(), held_as=jnp.bfloat16):
    array = deviation * jax.random.normal(stream_key, extent, jnp.float32)
    if shards:
        array = array * block_levels(stream_key, extent, shards, -0.22, 0.18)
    return jnp.clip(array, -most, most).astype(held_as)


def setup_inputs(seed: int = 0) -> dict:
    key_list = jax.random.split(jax.random.key(seed), 5)
    return {
        "volts": gaussian(key_list[0], (2, INPUTS, CHANNELS, SAMPLES), 1.0, 6.0, ((1, 512),)),
        "pfb_taps": gaussian(key_list[1], (TAPS, FINE), TAPS ** -0.5, 2.5, (), jnp.float32),
        "channel_order": jax.random.permutation(key_list[2], CHANNELS).astype(jnp.int32),
        "station_slot": jax.random.permutation(key_list[3], STATIONS).astype(jnp.int32),
    }


def dft_table(length):
    index = jnp.arange(length, dtype=jnp.int32)
    product = index[:, None] * index[None, :] % length
    angle = product.astype(jnp.float32) * (2.0 * math.pi / length)
    factor = 1.0 / math.sqrt(length)
    cosine = jnp.cos(angle) * factor
    sine = jnp.sin(angle) * factor
    upper = jnp.concatenate([cosine, -sine], 1)
    lower = jnp.concatenate([sine, cosine], 1)
    return jnp.concatenate([upper, lower], 0).astype(jnp.bfloat16)

def twiddle(first, second):
    total = first * second
    inner = jnp.arange(second, dtype=jnp.int32)
    outer = jnp.arange(first, dtype=jnp.int32)
    product = inner[:, None] * outer[None, :] % total
    angle = product.astype(jnp.float32) * (2.0 * math.pi / total)
    return (jnp.cos(angle), jnp.sin(angle))

def transform(stacked, first):
    rows = stacked.shape[0]
    fine = stacked.shape[1] // 2
    second = fine // first
    shaped = stacked.reshape(rows, 2, first, second)
    shaped = jnp.transpose(shaped, (0, 3, 1, 2)).reshape(rows, second, 2 * first)
    sectioned = jnp.einsum('rbk,kq->rbq', shaped.astype(jnp.float32), dft_table(first).astype(jnp.float32))
    real_part = sectioned[:, :, :first]
    imag_part = sectioned[:, :, first:]
    cosine, sine = twiddle(first, second)
    turned_re = real_part * cosine + imag_part * sine
    turned_im = imag_part * cosine - real_part * sine
    section = jnp.stack([turned_re, turned_im], 2).astype(jnp.bfloat16)
    section = jnp.transpose(section, (0, 3, 2, 1)).reshape(rows, first, 2 * second)
    result = jnp.einsum('rak,kq->raq', section.astype(jnp.float32), dft_table(second).astype(jnp.float32))
    result = result.reshape(rows, first, 2, second)
    result = jnp.transpose(result, (0, 2, 3, 1)).reshape(rows, 2 * fine)
    return result.astype(jnp.bfloat16)

def filterbank(volts, pfb_taps):
    two, count, chans, samples = volts.shape
    ntaps, fine = pfb_taps.shape
    frames_all = samples // fine
    spec = frames_all - ntaps + 1
    frames = volts.reshape(two, count, chans, frames_all, fine)
    filtered = jnp.zeros((two, count, chans, spec, fine), jnp.float32)
    for tap in range(ntaps):
        filtered = filtered + pfb_taps[tap].astype(jnp.float32) * frames[:, :, :, tap:tap + spec, :].astype(jnp.float32)
    filtered = filtered.astype(jnp.bfloat16)
    stacked = jnp.moveaxis(filtered, 0, 3).reshape(count * chans * spec, 2 * fine)
    spectra = transform(stacked, FA)
    return spectra.reshape(count, chans, spec, 2 * fine)

def cross_operands(spectra, group):
    count, chans, spec, width = spectra.shape
    fine = width // 2
    groups = fine // group
    parts = spectra.reshape(count, chans, spec, 2, groups, group)
    parts = jnp.transpose(parts, (3, 1, 4, 0, 2, 5)).reshape(2, chans, groups, count, spec * group)
    real_part = parts[0]
    imag_part = parts[1]
    right = jnp.concatenate([real_part, imag_part], -1)
    left = jnp.concatenate([right, jnp.concatenate([imag_part, -real_part], -1)], 2)
    return (left, right)

def column_source(station_slot):
    inputs = 2 * station_slot.shape[0]
    position = jnp.arange(inputs, dtype=jnp.int32)
    return (2 * jnp.take(station_slot, position // 2) + position % 2).astype(jnp.int32)

def reference(volts, pfb_taps, channel_order, station_slot):
    inverse = jnp.argsort(channel_order).astype(jnp.int32)
    columns = column_source(station_slot)

    def one_channel(slot):
        chan_volts = lax.dynamic_slice_in_dim(volts, slot, 1, 2)
        spectra = filterbank(chan_volts, pfb_taps)
        left, right = cross_operands(spectra, FGROUP)
        scale = 1.0 / (left.shape[-1] // 2)
        block = jnp.einsum('cgak,cgbk->cgab', left.astype(jnp.float32), right.astype(jnp.float32)) * scale
        block = block.reshape(1, OUTCH, 2, INPUTS, INPUTS)
        return jnp.take(block, columns, axis=4)[0]
    return lax.map(one_channel, inverse)
```

```python
import functools
import math

import jax
import jax.numpy as jnp
import numpy as np
from jax import lax
from jax.experimental import pallas as pl
from jax.experimental.pallas import tpu as pltpu
from jax.sharding import PartitionSpec as P

F32 = jnp.float32
BF16 = jnp.bfloat16
MESH = pl.DeviceIdType.MESH

TAPS = 6
FINE = 2048
N1 = 16
N2 = 128
CH = 32
Z = 8
PLANE = 2 * CH
HALF = 8
FAR = 4
PARTS = 8
SCALE = 2.0**-22


def tables():
    j2 = np.arange(N2)
    f1 = np.arange(N1)
    angle = 2 * math.pi * (f1[:, None] * j2[None, :]) / FINE
    twiddle = np.stack([np.cos(angle), np.sin(angle)]).astype(np.float32)
    theta = 2 * math.pi * (j2[:, None] * j2[None, :] % N2) / N2
    cosine, sine = np.cos(theta), np.sin(theta)
    full = np.zeros((2, N2, 2, 2, 64))
    for g in range(2):
        part = slice(64 * g, 64 * g + 64)
        full[0, :, g, 0] = cosine[:, part]
        full[1, :, g, 0] = sine[:, part]
        full[0, :, g, 1] = -sine[:, part]
        full[1, :, g, 1] = cosine[:, part]
    dft = full.reshape(256, 256).astype(jnp.bfloat16)
    shuffle = np.zeros((256, 256))
    for slot in range(16):
        for a in range(2):
            for f in range(HALF):
                shuffle[f * 32 + slot * 2 + a, slot * 16 + a * 8 + f] = 1
    turn = np.zeros((256, 256))
    for s in range(2):
        for f in range(64):
            turn[s * 128 + 64 + f, s * 128 + f] = 1
            turn[s * 128 + f, s * 128 + 64 + f] = -1
    return twiddle, dft, shuffle.astype(jnp.bfloat16), turn.astype(jnp.bfloat16)


def dft4(v):
    (ar, ai), (br, bi), (cr, ci), (dr, di) = v
    pr, pi, mr, mi = ar + cr, ai + ci, ar - cr, ai - ci
    qr, qi, nr, ni = br + dr, bi + di, br - dr, bi - di
    return [
        (pr + qr, pi + qi),
        (mr + ni, mi - nr),
        (pr - qr, pi - qi),
        (mr - ni, mi + nr),
    ]


def rotate(v, k):
    k = k % 16
    re, im = v
    if k == 0:
        return v
    if k == 4:
        return im, -re
    c, s = math.cos(2 * math.pi * k / 16), math.sin(2 * math.pi * k / 16)
    if k == 2:
        return (re + im) * c, (im - re) * c
    if k == 6:
        return (im - re) * s, (re + im) * -s
    return re * c + im * s, im * c - re * s


def dft16(x):
    inner = [dft4([x[4 * n + m] for n in range(4)]) for m in range(4)]
    out = [None] * 16
    for k in range(4):
        column = dft4([rotate(inner[m][k], m * k) for m in range(4)])
        for q in range(4):
            out[k + 4 * q] = column[q]
    return out


def spectra_kernel(volts, taps, order, twiddle, dft, out, section, mover, first):
    a = pl.program_id(0)

    @pl.when(a == 0)
    def _():
        spread = lax.broadcasted_iota(jnp.int32, (CH, 512), 1) % CH
        spread = spread == lax.broadcasted_iota(jnp.int32, (CH, 512), 0)
        rows = jnp.broadcast_to(order[...], (8, CH)).astype(F32).astype(BF16)
        goal = jnp.dot(rows, spread.astype(F32).astype(BF16), preferred_element_type=F32)[0:1]
        row = lax.broadcasted_iota(jnp.int32, (512, 512), 0)
        col = lax.broadcasted_iota(jnp.int32, (512, 512), 1)
        same = (row // N1 == goal.astype(jnp.int32)) & (row % N1 == col // CH)
        mover[...] = same.astype(F32).astype(BF16)

    for s in range(2):
        for h in range(2):
            rows = pl.ds(h * 16, 16)

            def point(p, j):
                total = None
                for t in range(TAPS):
                    at = (s + t) * FINE + j * N2
                    term = taps[t : t + 1, j * N2 : (j + 1) * N2] * volts[
                        p, 0, rows, at : at + N2
                    ].astype(F32)
                    total = term if total is None else total + term
                return total.astype(BF16).astype(F32)

            x = [(point(0, j), point(1, j)) for j in range(N1)]
            for f, (re, im) in enumerate(dft16(x)):
                c, d = twiddle[0, f : f + 1], twiddle[1, f : f + 1]
                at = pl.ds(f * CH + h * 16, 16)
                section[at, 0:N2] = (re * c + im * d).astype(BF16)
                section[at, N2 : 2 * N2] = (im * c - re * d).astype(BF16)
        moved = jnp.dot(mover[...], section[...], preferred_element_type=F32).astype(BF16)
        result = jnp.dot(moved, dft[...], preferred_element_type=F32)
        result = result.reshape(CH, 2, HALF, 256)

        @pl.when(a == 0)
        def _():
            first[s] = result

        @pl.when(a == 1)
        def _():
            other = first[s]
            for h in range(2):
                both = jnp.concatenate([other[:, h], result[:, h]], axis=1).astype(BF16)
                for g in range(2):
                    out[h, g, :, :, s * 128 : (s + 1) * 128] = both[:, :, g * 128 : (g + 1) * 128]


def spectra(volts, taps, order, twiddle, dft):
    samples = volts.shape[-1]
    return pl.pallas_call(
        spectra_kernel,
        grid=(2,),
        out_shape=jax.ShapeDtypeStruct((2, 2, CH, 16, 256), BF16),
        in_specs=[
            pl.BlockSpec((2, 1, CH, samples), lambda a: (0, a, 0, 0)),
            pl.BlockSpec((TAPS, FINE), lambda a: (0, 0)),
            pl.BlockSpec((1, CH), lambda a: (0, 0)),
            pl.BlockSpec((2, N1, N2), lambda a: (0, 0, 0)),
            pl.BlockSpec((256, 256), lambda a: (0, 0)),
        ],
        out_specs=pl.BlockSpec((2, 2, CH, 16, 256), lambda a: (0, 0, 0, 0, 0)),
        scratch_shapes=[
            pltpu.VMEM((512, 256), BF16),
            pltpu.VMEM((512, 512), BF16),
            pltpu.VMEM((2, CH, 2, HALF, 256), F32),
        ],
        compiler_params=pltpu.CompilerParams(vmem_limit_bytes=40 * 2**20),
        name="spectra",
    )(volts, taps, order, twiddle, dft)


def cross_kernel(
    sent, slots, shuffle, turn, out,
    arrived, blocks, left, total, places, final, partner, mirror,
    own_sem, turn_send, turn_recv, ring_send, ring_recv,
    final_recv, partner_send, mirror_send,
):
    chan = lax.axis_index("chan")
    inp = lax.axis_index("inp")
    g = inp // Z
    z = inp % Z
    me = g * CH + chan
    way = 1 - 2 * (chan % 2)

    def along(hops):
        return (z + hops * way + Z) % Z

    def in_plane(k):
        peer = (me + k) % PLANE
        return peer, (peer % CH, (peer // CH) * Z + z)

    barrier = pltpu.get_barrier_semaphore()

    def greet_plane(k, _):
        pl.semaphore_signal(barrier, inc=1, device_id=in_plane(k)[1], device_id_type=MESH)
        return 0

    def greet_column(k, _):
        there = (z + k) % Z
        for x in range(2):
            pl.semaphore_signal(
                barrier, inc=1, device_id=(chan, x * Z + there), device_id_type=MESH
            )
        return 0

    lax.fori_loop(1, PLANE, greet_plane, 0)
    lax.fori_loop(1, Z, greet_column, 0)
    pl.semaphore_wait(barrier, PLANE - 1 + 2 * (Z - 1))

    for h in range(2):
        pltpu.make_async_copy(sent.at[h, me], arrived.at[h, me], own_sem.at[h]).start()

        def send(k, _):
            peer, device = in_plane(k)
            pltpu.make_async_remote_copy(
                src_ref=sent.at[h, peer],
                dst_ref=arrived.at[h, me],
                send_sem=turn_send.at[h],
                recv_sem=turn_recv.at[h],
                device_id=device,
                device_id_type=MESH,
            ).start()
            return 0

        lax.fori_loop(1, PLANE, send, 0)

    def one_hot(e, _):
        value = jnp.broadcast_to(slots[...], (8, 512))
        spread = lax.broadcasted_iota(jnp.int32, (512, 1024), 1) // 2
        spread = spread == lax.broadcasted_iota(jnp.int32, (512, 1024), 0)
        spread = spread.astype(F32).astype(BF16)
        high = jnp.dot((value // 32).astype(F32).astype(BF16), spread, preferred_element_type=F32)
        low = jnp.dot((value % 32).astype(F32).astype(BF16), spread, preferred_element_type=F32)
        station = (high * 32.0 + low)[0:1].astype(jnp.int32)
        source = 2 * station + lax.broadcasted_iota(jnp.int32, (1, 1024), 1) % 2
        row = lax.broadcasted_iota(jnp.int32, (128, 1), 0)
        row = (row // 64) * (64 * Z) + row % 64 + along(-e) * 64
        places[e] = (source == row).astype(F32).astype(BF16)
        return 0

    lax.fori_loop(0, 8, one_hot, 0)

    def piece(ref, d, q):
        return ref.at[d, pl.ds(q * 2, 2)]

    def pass_on(d, q):
        return pltpu.make_async_remote_copy(
            src_ref=piece(blocks, d, q),
            dst_ref=piece(blocks, d + 1, q),
            send_sem=ring_send.at[d, q],
            recv_sem=ring_recv.at[d, q],
            device_id=(chan, g * Z + along(1)),
            device_id_type=MESH,
        )

    def multiply(d, f):
        total[...] += lax.dot_general(
            left[f], blocks[d, f], (((1,), (1,)), ((), ())), preferred_element_type=F32
        )

    def to_partner(d):
        return pltpu.make_async_remote_copy(
            src_ref=partner.at[d],
            dst_ref=final.at[d, g],
            send_sem=partner_send.at[d],
            recv_sem=final_recv.at[d, g],
            device_id=(chan, (1 - g) * Z + z),
            device_id_type=MESH,
        )

    def to_column(d, x):
        return pltpu.make_async_remote_copy(
            src_ref=mirror.at[d, x],
            dst_ref=final.at[8 - d, g],
            send_sem=mirror_send.at[d, x],
            recv_sem=final_recv.at[8 - d, g],
            device_id=(chan, x * Z + along(-d)),
            device_id_type=MESH,
        )

    def finish(d):
        for p in range(2):
            mine = pl.ds(pl.multiple_of(p * 128 + g * 64, 64), 64)
            other = pl.ds(pl.multiple_of(p * 128 + (1 - g) * 64, 64), 64)
            final[d, g, p] = total[mine, :].astype(BF16)
            partner[d, p] = total[other, :].astype(BF16)
        to_partner(d).start()

    for h in range(2):
        pltpu.make_async_copy(sent.at[h, me], arrived.at[h, me], own_sem.at[h]).wait()
        several = arrived.at[h, pl.ds(0, PLANE - 1)]
        pltpu.make_async_copy(several, several, turn_recv.at[h]).wait()

        def arrange(q, _):
            rows = arrived[h, pl.ds(q * 16, 16)].reshape(256, 256)
            rows = jnp.dot(shuffle[...], rows, preferred_element_type=F32).astype(BF16)
            turned = jnp.dot(rows, turn[...], preferred_element_type=F32).astype(BF16)
            at = pl.ds(pl.multiple_of(q * 32, 32), 32)
            low = pl.ds(pl.multiple_of(q * 32 + 128, 32), 32)
            several = pl.ds(h * HALF, HALF)
            blocks[0, several, at, :] = rows.reshape(HALF, 32, 256)
            left[several, at, :] = rows.reshape(HALF, 32, 256)
            left[several, low, :] = turned.reshape(HALF, 32, 256)
            return 0

        lax.fori_loop(0, PLANE // 16, arrange, 0)

        def start(q, _):
            pass_on(0, q).start()
            return 0

        lax.fori_loop(h * PARTS // 2, (h + 1) * PARTS // 2, start, 0)

    total[...] = jnp.zeros_like(total)

    def own(f, _):
        multiply(0, f)
        return 0

    lax.fori_loop(0, N1, own, 0)
    finish(0)

    def hop(d, _):
        total[...] = jnp.zeros_like(total)

        def step(q, _):
            pass_on(d - 1, q).wait_recv()

            @pl.when(d < FAR)
            def _():
                pass_on(d, q).start()

            multiply(d, 2 * q)
            multiply(d, 2 * q + 1)
            return 0

        lax.fori_loop(0, PARTS, step, 0)
        finish(d)

        @pl.when(d < FAR)
        def _():
            re = total[0:128, :].T
            im = -total[128:256, :].T
            for x in range(2):
                mirror[d, x, 0] = re[x * 64 : (x + 1) * 64].astype(BF16)
                mirror[d, x, 1] = im[x * 64 : (x + 1) * 64].astype(BF16)
                to_column(d, x).start()

        return 0

    lax.fori_loop(1, FAR + 1, hop, 0)

    def from_partner(d, _):
        there = final.at[d, 1 - g]
        pltpu.make_async_copy(there, there, final_recv.at[d, 1 - g]).wait()
        return 0

    lax.fori_loop(0, FAR + 1, from_partner, 0)

    def from_column(d, _):
        for x in range(2):
            there = final.at[8 - d, x]
            pltpu.make_async_copy(there, there, final_recv.at[8 - d, x]).wait()
        return 0

    lax.fori_loop(1, FAR, from_column, 0)

    for n in range(4):
        columns = slice(n * 256, (n + 1) * 256)
        tile = jnp.zeros((256, 256), F32)
        for e in range(8):
            tile += jnp.dot(
                final[e].reshape(256, 128), places[e, :, columns], preferred_element_type=F32
            )
        out[0, :, :, :, columns] = (tile * SCALE).reshape(2, 2, 64, 256)

    for h in range(2):
        several = sent.at[h, pl.ds(0, PLANE - 1)]
        pltpu.make_async_copy(several, several, turn_send.at[h]).wait()

    def drain(d, _):
        to_partner(d).wait_send()

        @pl.when(d < FAR)
        def _():
            def one(q, _):
                pass_on(d, q).wait_send()
                return 0

            lax.fori_loop(0, PARTS, one, 0)

            @pl.when(d > 0)
            def _():
                for x in range(2):
                    to_column(d, x).wait_send()

        return 0

    lax.fori_loop(0, FAR + 1, drain, 0)


def cross(sent, slots, shuffle, turn):
    dma = pltpu.SemaphoreType.DMA
    return pl.pallas_call(
        cross_kernel,
        out_shape=jax.ShapeDtypeStruct((1, 2, 2, 64, 1024), F32),
        in_specs=[pl.BlockSpec(memory_space=pl.ANY)] + [pl.BlockSpec(memory_space=pltpu.VMEM)] * 3,
        out_specs=pl.BlockSpec(memory_space=pltpu.VMEM),
        scratch_shapes=[
            pltpu.VMEM((2, PLANE, 16, 256), BF16),
            pltpu.VMEM((FAR + 1, N1, 128, 256), BF16),
            pltpu.VMEM((N1, 256, 256), BF16),
            pltpu.VMEM((256, 128), F32),
            pltpu.VMEM((8, 128, 1024), BF16),
            pltpu.VMEM((8, 2, 2, 64, 128), BF16),
            pltpu.VMEM((FAR + 1, 2, 64, 128), BF16),
            pltpu.VMEM((FAR, 2, 2, 64, 128), BF16),
            dma((2,)),
            dma((2,)),
            dma((2,)),
            dma((FAR, PARTS)),
            dma((FAR, PARTS)),
            dma((8, 2)),
            dma((FAR + 1,)),
            dma((FAR, 2)),
        ],
        compiler_params=pltpu.CompilerParams(
            collective_id=0, has_side_effects=True, vmem_limit_bytes=40 * 2**20
        ),
        name="cross",
    )(sent, slots, shuffle, turn)


def local(volts, pfb_taps, channel_order, station_slot):
    twiddle, dft, shuffle, turn = tables()
    result = spectra(volts, pfb_taps, channel_order.reshape(1, CH), twiddle, dft)
    sent = result.reshape(2, PLANE, 16, 256)
    return cross(sent, station_slot.reshape(1, -1), shuffle, turn)


def solution(mesh):
    in_specs = (P(None, ("inp", "chan"), None, None), P(), P(), P())
    out_specs = P("chan", None, None, "inp", None)
    return jax.shard_map(local, mesh=mesh, in_specs=in_specs, out_specs=out_specs, check_vma=False)
```

```python
import functools
import math

import jax
import jax.numpy as jnp
import numpy as np
from jax import lax
from jax.experimental import pallas as pl
from jax.experimental.pallas import tpu as pltpu
from jax.sharding import PartitionSpec as P

F32 = jnp.float32
BF16 = jnp.bfloat16
MESH = pl.DeviceIdType.MESH

TAPS = 6
FINE = 2048
N1 = 16
N2 = 128
CH = 32
Z = 8
PLANE = 2 * CH
HALF = 8
QUARTERS = 4
DEEP = 4
FAR = 4
PIECES = 2
SCALE = 2.0**-22


def tables():
    j2 = np.arange(N2)
    f1 = np.arange(N1)
    angle = 2 * math.pi * (f1[:, None] * j2[None, :]) / FINE
    twiddle = np.stack([np.cos(angle), np.sin(angle)]).astype(np.float32)
    theta = 2 * math.pi * (j2[:, None] * j2[None, :] % N2) / N2
    cosine, sine = np.cos(theta), np.sin(theta)
    full = np.zeros((2, N2, 2, 2, 64))
    for g in range(2):
        part = slice(64 * g, 64 * g + 64)
        full[0, :, g, 0] = cosine[:, part]
        full[1, :, g, 0] = sine[:, part]
        full[0, :, g, 1] = -sine[:, part]
        full[1, :, g, 1] = cosine[:, part]
    dft = full.reshape(256, 256).astype(jnp.bfloat16)
    shuffle = np.zeros((256, 256))
    for slot in range(16):
        for a in range(2):
            for f in range(HALF):
                shuffle[f * 32 + slot * 2 + a, slot * 16 + a * 8 + f] = 1
    turn = np.zeros((256, 256))
    for s in range(2):
        for f in range(64):
            turn[s * 128 + 64 + f, s * 128 + f] = 1
            turn[s * 128 + f, s * 128 + 64 + f] = -1
    return twiddle, dft, shuffle.astype(jnp.bfloat16), turn.astype(jnp.bfloat16)


def dft4(v):
    (ar, ai), (br, bi), (cr, ci), (dr, di) = v
    pr, pi, mr, mi = ar + cr, ai + ci, ar - cr, ai - ci
    qr, qi, nr, ni = br + dr, bi + di, br - dr, bi - di
    return [
        (pr + qr, pi + qi),
        (mr + ni, mi - nr),
        (pr - qr, pi - qi),
        (mr - ni, mi + nr),
    ]


def rotate(v, k):
    k = k % 16
    re, im = v
    if k == 0:
        return v
    if k == 4:
        return im, -re
    c, s = math.cos(2 * math.pi * k / 16), math.sin(2 * math.pi * k / 16)
    if k == 2:
        return (re + im) * c, (im - re) * c
    if k == 6:
        return (im - re) * s, (re + im) * -s
    return re * c + im * s, im * c - re * s


def dft16(x):
    inner = [dft4([x[4 * n + m] for n in range(4)]) for m in range(4)]
    out = [None] * 16
    for k in range(4):
        column = dft4([rotate(inner[m][k], m * k) for m in range(4)])
        for q in range(4):
            out[k + 4 * q] = column[q]
    return out


SENDS = 4
LATE = (FAR, FAR + 1)
ORDER = (
    [("send", 1, n) for n in range(SENDS)]
    + [("columns",), ("take", 0)] + [("send", 2, n) for n in range(SENDS)]
    + [("pass", 1, 0), ("take", 1)] + [("send", 3, n) for n in range(SENDS)]
    + [("pass", 2, 0), ("pass", 1, 1), ("pass", 2, 1)]
    + [("take", 2), ("pass", 1, 2), ("take", 3), ("pass", 2, 2), ("pass", 1, 3), ("pass", 2, 3)]
    + [("pass", 3, q) for q in range(QUARTERS)]
    + [("pass", 4, 0), ("pass", 4, 1), ("product",), ("pass", 4, 2), ("pass", 4, 3)]
)


def cross_kernel(
    volts_hbm, taps_hbm, order_hbm, slots_hbm, twiddle_hbm, dft_hbm, shuffle_hbm, turn_hbm, out,
    volts, taps, order, slots, twiddle, dft, shuffle, turn,
    section, mover, first, sent, arrived, blocks, left, total, places, sums, final, partner, mirror,
    volts_sem, small_sem, own_sem, turn_send, turn_recv, ring_send, ring_recv,
    final_recv, partner_send, mirror_send,
):
    chan = lax.axis_index("chan")
    inp = lax.axis_index("inp")
    g = lax.div(inp, Z)
    z = lax.rem(inp, Z)
    me = g * CH + chan
    way = 1 - 2 * lax.rem(chan, 2)

    def along(hops):
        return lax.rem(z + hops * way + Z, Z)

    def peers(act, n=0, parts=1):
        step = CH // 2 // parts
        if n == 0:
            act(1 - g, chan)

        def one(k, _):
            for c in (lax.rem(chan + k, CH), lax.rem(chan + CH - k, CH)):
                act(g, c)
                act(1 - g, c)
            return 0

        lax.fori_loop(max(n * step, 1), (n + 1) * step, one, 0)
        if n == parts - 1:
            far = lax.rem(chan + CH // 2, CH)
            act(g, far)
            act(1 - g, far)

    small = [
        pltpu.make_async_copy(source, target, small_sem.at[n])
        for n, (source, target) in enumerate(
            [
                (order_hbm, order), (taps_hbm, taps), (twiddle_hbm, twiddle), (dft_hbm, dft),
                (slots_hbm, slots), (shuffle_hbm, shuffle), (turn_hbm, turn),
            ]
        )
    ]
    large = [
        [
            pltpu.make_async_copy(volts_hbm.at[p, a], volts.at[a, p], volts_sem.at[a, p])
            for p in range(2)
        ]
        for a in range(2)
    ]
    small[0].start()
    for copy in large[0] + small[1:4] + large[1] + small[4:]:
        copy.start()

    barrier = pltpu.get_barrier_semaphore()

    def greet(x, c):
        pl.semaphore_signal(barrier, inc=1, device_id=(c, x * Z + z), device_id_type=MESH)

    def greet_column(k, _):
        there = lax.rem(z + k, Z)
        for x in range(2):
            pl.semaphore_signal(
                barrier, inc=1, device_id=(chan, x * Z + there), device_id_type=MESH
            )
        return 0

    peers(greet)
    lax.fori_loop(1, Z, greet_column, 0)

    small[0].wait()
    spread = lax.broadcasted_iota(jnp.int32, (CH, 512), 1) % CH
    spread = spread == lax.broadcasted_iota(jnp.int32, (CH, 512), 0)
    rows = jnp.broadcast_to(order[...], (8, CH)).astype(F32).astype(BF16)
    goal = jnp.dot(rows, spread.astype(F32).astype(BF16), preferred_element_type=F32)[0:1]
    row = lax.broadcasted_iota(jnp.int32, (512, 512), 0)
    col = lax.broadcasted_iota(jnp.int32, (512, 512), 1)
    same = (row // N1 == goal.astype(jnp.int32)) & (row % N1 == col // CH)
    mover[...] = same.astype(F32).astype(BF16)

    def transform(s, a):
        for h in range(2):
            rows = pl.ds(h * 16, 16)

            def point(p, j):
                total = None
                for t in range(TAPS):
                    at = (s + t) * FINE + j * N2
                    term = taps[t : t + 1, j * N2 : (j + 1) * N2] * volts[
                        a, p, rows, at : at + N2
                    ].astype(F32)
                    total = term if total is None else total + term
                return total.astype(BF16).astype(F32)

            x = [(point(0, j), point(1, j)) for j in range(N1)]
            for f, (re, im) in enumerate(dft16(x)):
                c, d = twiddle[0, f : f + 1], twiddle[1, f : f + 1]
                at = pl.ds(f * CH + h * 16, 16)
                section[a, at, 0:N2] = (re * c + im * d).astype(BF16)
                section[a, at, N2 : 2 * N2] = (im * c - re * d).astype(BF16)
        moved = jnp.dot(mover[...], section[a], preferred_element_type=F32).astype(BF16)
        result = jnp.dot(moved, dft[...], preferred_element_type=F32)
        return result.reshape(CH, 2, HALF, 256)

    def spectrum(s):
        if s == 0:
            for copy in small[1:4] + large[0]:
                copy.wait()
        first[...] = transform(s, 0)
        if s == 0:
            for copy in large[1]:
                copy.wait()
        second = transform(s, 1)
        for h in range(2):
            both = jnp.concatenate([first[:, h], second[:, h]], axis=1).astype(BF16)
            for k in range(2):
                sent[2 * s + h, k * CH : (k + 1) * CH] = both[:, :, k * 128 : (k + 1) * 128]

    def keep(q):
        return pltpu.make_async_copy(sent.at[q, me], arrived.at[q, me], own_sem.at[q])

    def send(q, n):
        def one(x, c):
            pltpu.make_async_remote_copy(
                src_ref=sent.at[q, x * CH + c],
                dst_ref=arrived.at[q, me],
                send_sem=turn_send.at[q],
                recv_sem=turn_recv.at[q],
                device_id=(c, x * Z + z),
                device_id_type=MESH,
            ).start()

        peers(one, n, SENDS)

    def columns():
        for copy in small[4:]:
            copy.wait()
        value = jnp.broadcast_to(slots[...], (8, 512))
        spread = lax.broadcasted_iota(jnp.int32, (512, 1024), 1) // 2
        spread = spread == lax.broadcasted_iota(jnp.int32, (512, 1024), 0)
        spread = spread.astype(F32).astype(BF16)
        high = jnp.dot((value // 32).astype(F32).astype(BF16), spread, preferred_element_type=F32)
        low = jnp.dot((value % 32).astype(F32).astype(BF16), spread, preferred_element_type=F32)
        station = (high * 32.0 + low)[0:1].astype(jnp.int32)
        source = 2 * station + lax.broadcasted_iota(jnp.int32, (1, 1024), 1) % 2

        def one_hot(e, _):
            row = lax.broadcasted_iota(jnp.int32, (128, 1), 0)
            row = (row // 64) * (64 * Z) + row % 64 + along(-e) * 64
            places[e] = (source == row).astype(F32).astype(BF16)
            return 0

        lax.fori_loop(0, 8, one_hot, 0)

    def pass_on(d, n):
        several = pl.ds(n * (DEEP // PIECES), DEEP // PIECES)
        return pltpu.make_async_remote_copy(
            src_ref=blocks.at[d, several],
            dst_ref=blocks.at[d + 1, several],
            send_sem=ring_send.at[d, n],
            recv_sem=ring_recv.at[d, n],
            device_id=(chan, g * Z + along(1)),
            device_id_type=MESH,
        )

    def multiply(d, start, count):
        value = None
        for k in range(count):
            term = lax.dot_general(
                left[start + k],
                blocks[d, start + k],
                (((1,), (1,)), ((), ())),
                preferred_element_type=F32,
            )
            value = term if value is None else value + term
        total[d] += value

    def take(q):
        keep(q).wait()
        several = arrived.at[q, pl.ds(0, PLANE - 1)]
        pltpu.make_async_copy(several, several, turn_recv.at[q]).wait()

        def arrange(n, _):
            rows = arrived[q, pl.ds(n * 16, 16)].reshape(256, 128)
            rows = jnp.dot(shuffle[...], rows, preferred_element_type=F32)
            rows = rows.reshape(DEEP, 2, 32, 128)
            rows = jnp.concatenate([rows[:, 0], rows[:, 1]], axis=-1).astype(BF16)
            turned = jnp.dot(rows.reshape(DEEP * 32, 256), turn[...], preferred_element_type=F32)
            at = pl.ds(pl.multiple_of(n * 32, 32), 32)
            low = pl.ds(pl.multiple_of(n * 32 + 128, 32), 32)
            several = pl.ds(q * DEEP, DEEP)
            blocks[0, several, at, :] = rows
            left[several, at, :] = rows
            left[several, low, :] = turned.astype(BF16).reshape(DEEP, 32, 256)
            return 0

        lax.fori_loop(0, PLANE // 16, arrange, 0)
        for n in range(PIECES):
            pass_on(0, q * PIECES + n).start()
        multiply(0, q * DEEP, DEEP)

    def receive(d, q):
        def one(n, _):
            pass_on(d - 1, n).wait_recv()
            if d < FAR:
                pass_on(d, n).start()
            multiply(d, n * (DEEP // PIECES), DEEP // PIECES)
            return 0

        lax.fori_loop(q * PIECES, (q + 1) * PIECES, one, 0)

    def to_partner(d):
        return pltpu.make_async_remote_copy(
            src_ref=partner.at[d],
            dst_ref=final.at[d, g],
            send_sem=partner_send.at[d],
            recv_sem=final_recv.at[d, g],
            device_id=(chan, (1 - g) * Z + z),
            device_id_type=MESH,
        )

    def to_column(d, x):
        return pltpu.make_async_remote_copy(
            src_ref=mirror.at[d, x],
            dst_ref=final.at[8 - d, g],
            send_sem=mirror_send.at[d, x],
            recv_sem=final_recv.at[8 - d, g],
            device_id=(chan, x * Z + along(-d)),
            device_id_type=MESH,
        )

    def finish(d):
        for p in range(2):
            mine = pl.ds(pl.multiple_of(p * 128 + g * 64, 64), 64)
            other = pl.ds(pl.multiple_of(p * 128 + (1 - g) * 64, 64), 64)
            final[d, g, p] = total[d, mine, :].astype(BF16)
            partner[d, p] = total[d, other, :].astype(BF16)
        to_partner(d).start()
        if 0 < d < FAR:
            re = total[d, 0:128, :].T
            im = -total[d, 128:256, :].T
            for x in range(2):
                mirror[d, x, 0] = re[x * 64 : (x + 1) * 64].astype(BF16)
                mirror[d, x, 1] = im[x * 64 : (x + 1) * 64].astype(BF16)
                to_column(d, x).start()

    def placed(e, n):
        columns = slice(n * 256, (n + 1) * 256)
        return jnp.dot(
            final[e].reshape(256, 128), places[e, :, columns], preferred_element_type=F32
        )

    def arrives(e, x):
        there = final.at[e, x]
        pltpu.make_async_copy(there, there, final_recv.at[e, x]).wait()

    def product():
        for e in range(8):
            if e < FAR:
                arrives(e, 1 - g)
            if e > FAR + 1:
                arrives(e, 0)
                arrives(e, 1)
        for n in range(4):
            tile = placed(0, n)
            for e in range(1, 8):
                if e not in LATE:
                    tile += placed(e, n)
            sums[n] = tile

    total[...] = jnp.zeros_like(total)
    spectrum(0)
    pl.semaphore_wait(barrier, PLANE - 1 + 2 * (Z - 1))
    for q in (0, 1):
        keep(q).start()
    for n in range(SENDS):
        send(0, n)
    spectrum(1)
    for q in (2, 3):
        keep(q).start()
    for what, *which in ORDER:
        if what == "send":
            send(*which)
        elif what == "take":
            take(*which)
            if which[0] == QUARTERS - 1:
                finish(0)
        elif what == "pass":
            receive(*which)
            if which[1] == QUARTERS - 1:
                finish(which[0])
        elif what == "columns":
            columns()
        else:
            product()
    arrives(FAR + 1, 0)
    arrives(FAR + 1, 1)
    arrives(FAR, 1 - g)
    for n in range(4):
        tile = (sums[n] + placed(FAR + 1, n) + placed(FAR, n)) * SCALE
        out[0, :, :, :, n * 256 : (n + 1) * 256] = tile.reshape(2, 2, 64, 256)

    for q in range(QUARTERS):
        several = sent.at[q, pl.ds(0, PLANE - 1)]
        pltpu.make_async_copy(several, several, turn_send.at[q]).wait()

    def drain(d, _):
        def one(n, _):
            pass_on(d, n).wait_send()
            return 0

        lax.fori_loop(0, QUARTERS * PIECES, one, 0)
        return 0

    lax.fori_loop(0, FAR, drain, 0)
    for d in range(FAR + 1):
        to_partner(d).wait_send()
        if 0 < d < FAR:
            for x in range(2):
                to_column(d, x).wait_send()


def cross(*operands):
    dma = pltpu.SemaphoreType.DMA
    return pl.pallas_call(
        cross_kernel,
        out_shape=jax.ShapeDtypeStruct((1, 2, 2, 64, 1024), F32),
        in_specs=[pl.BlockSpec(memory_space=pl.ANY)] * 8,
        out_specs=pl.BlockSpec(memory_space=pltpu.VMEM),
        scratch_shapes=[
            pltpu.VMEM((2, 2, CH, 7 * FINE), BF16),
            pltpu.VMEM((TAPS, FINE), F32),
            pltpu.VMEM((1, CH), jnp.int32),
            pltpu.VMEM((1, 512), jnp.int32),
            pltpu.VMEM((2, N1, N2), F32),
            pltpu.VMEM((256, 256), BF16),
            pltpu.VMEM((256, 256), BF16),
            pltpu.VMEM((256, 256), BF16),
            pltpu.VMEM((2, 512, 256), BF16),
            pltpu.VMEM((512, 512), BF16),
            pltpu.VMEM((CH, 2, HALF, 256), F32),
            pltpu.VMEM((QUARTERS, PLANE, 16, 128), BF16),
            pltpu.VMEM((QUARTERS, PLANE, 16, 128), BF16),
            pltpu.VMEM((FAR + 1, QUARTERS * DEEP, 128, 256), BF16),
            pltpu.VMEM((QUARTERS * DEEP, 256, 256), BF16),
            pltpu.VMEM((FAR + 1, 256, 128), F32),
            pltpu.VMEM((8, 128, 1024), BF16),
            pltpu.VMEM((4, 256, 256), F32),
            pltpu.VMEM((8, 2, 2, 64, 128), BF16),
            pltpu.VMEM((FAR + 1, 2, 64, 128), BF16),
            pltpu.VMEM((FAR, 2, 2, 64, 128), BF16),
            dma((2, 2)),
            dma((7,)),
            dma((QUARTERS,)),
            dma((QUARTERS,)),
            dma((QUARTERS,)),
            dma((FAR, QUARTERS * PIECES)),
            dma((FAR, QUARTERS * PIECES)),
            dma((8, 2)),
            dma((FAR + 1,)),
            dma((FAR, 2)),
        ],
        compiler_params=pltpu.CompilerParams(
            collective_id=0, has_side_effects=True, vmem_limit_bytes=60 * 2**20
        ),
        name="cross",
    )(*operands)


def local(volts, pfb_taps, channel_order, station_slot):
    order, slots = channel_order.reshape(1, CH), station_slot.reshape(1, -1)
    return cross(volts, pfb_taps, order, slots, *tables())


def solution(mesh):
    in_specs = (P(None, ("inp", "chan"), None, None), P(), P(), P())
    out_specs = P("chan", None, None, "inp", None)
    return jax.shard_map(local, mesh=mesh, in_specs=in_specs, out_specs=out_specs, check_vma=False)
```

```python
import functools
import math

import jax
import jax.numpy as jnp
import numpy as np
from jax import lax
from jax.experimental import pallas as pl
from jax.experimental.pallas import tpu as pltpu
from jax.sharding import PartitionSpec as P

F32 = jnp.float32
BF16 = jnp.bfloat16
MESH = pl.DeviceIdType.MESH

TAPS = 6
FINE = 2048
N1 = 16
N2 = 128
CH = 32
Z = 8
PLANE = 2 * CH
HALF = 8
QUARTERS = 4
DEEP = 4
FAR = 4
DEPTH = 3
PIECES = 2
SCALE = 2.0**-22


def tables():
    j2 = np.arange(N2)
    f1 = np.arange(N1)
    angle = 2 * math.pi * (f1[:, None] * j2[None, :]) / FINE
    twiddle = np.stack([np.cos(angle), np.sin(angle)]).astype(np.float32)
    theta = 2 * math.pi * (j2[:, None] * j2[None, :] % N2) / N2
    cosine, sine = np.cos(theta), np.sin(theta)
    full = np.zeros((2, N2, 2, 2, 64))
    for g in range(2):
        part = slice(64 * g, 64 * g + 64)
        full[0, :, g, 0] = cosine[:, part]
        full[1, :, g, 0] = sine[:, part]
        full[0, :, g, 1] = -sine[:, part]
        full[1, :, g, 1] = cosine[:, part]
    dft = full.reshape(256, 256).astype(jnp.bfloat16)
    shuffle = np.zeros((256, 256))
    for slot in range(16):
        for a in range(2):
            for f in range(HALF):
                shuffle[f * 32 + slot * 2 + a, slot * 16 + a * 8 + f] = 1
    turn = np.zeros((256, 256))
    for s in range(2):
        for f in range(64):
            turn[s * 128 + 64 + f, s * 128 + f] = 1
            turn[s * 128 + f, s * 128 + 64 + f] = -1
    return twiddle, dft, shuffle.astype(jnp.bfloat16), turn.astype(jnp.bfloat16)


def dft4(v):
    (ar, ai), (br, bi), (cr, ci), (dr, di) = v
    pr, pi, mr, mi = ar + cr, ai + ci, ar - cr, ai - ci
    qr, qi, nr, ni = br + dr, bi + di, br - dr, bi - di
    return [
        (pr + qr, pi + qi),
        (mr + ni, mi - nr),
        (pr - qr, pi - qi),
        (mr - ni, mi + nr),
    ]


def rotate(v, k):
    k = k % 16
    re, im = v
    if k == 0:
        return v
    if k == 4:
        return im, -re
    c, s = math.cos(2 * math.pi * k / 16), math.sin(2 * math.pi * k / 16)
    if k == 2:
        return (re + im) * c, (im - re) * c
    if k == 6:
        return (im - re) * s, (re + im) * -s
    return re * c + im * s, im * c - re * s


def dft16(x):
    inner = [dft4([x[4 * n + m] for n in range(4)]) for m in range(4)]
    out = [None] * 16
    for k in range(4):
        column = dft4([rotate(inner[m][k], m * k) for m in range(4)])
        for q in range(4):
            out[k + 4 * q] = column[q]
    return out


SENDS = 2
LATE = (FAR, FAR + 1)
REST = 8
ORDER = (
    [("send", q, n) for q in (2, 3) for n in range(SENDS)]
    + [("columns",), ("take", 0), ("pass", 1, 0), ("take", 1), ("pass", 2, 0), ("pass", 1, 1)]
    + [("take", 2), ("pass", 2, 1), ("take", 3), ("pass", 1, 2), ("pass", 3, 0), ("pass", 1, 3)]
    + [("pass", 3, 1), ("pass", 2, 2), ("pass", 2, 3), ("pass", 3, 2), ("pass", 3, 3)]
    + [("pass", 4, 0), ("pass", 4, 1), ("product",), ("pass", 4, 2), ("pass", 4, 3)]
)


def cross_kernel(
    volts_hbm, taps_hbm, order_hbm, slots_hbm, twiddle_hbm, dft_hbm, shuffle_hbm, turn_hbm, out,
    volts, taps, order, slots, twiddle, dft, shuffle, turn,
    section, mover, first, sent, arrived, blocks, left, total, places, sums, final, partner, mirror,
    volts_sem, small_sem, own_sem, turn_send, turn_recv, ring_send, ring_recv,
    final_recv, partner_send, mirror_send,
):
    chan = lax.axis_index("chan")
    inp = lax.axis_index("inp")
    g = lax.div(inp, Z)
    z = lax.rem(inp, Z)
    me = g * CH + chan
    way = 1 - 2 * lax.rem(chan, 2)

    def along(hops):
        return lax.rem(z + hops * way + Z, Z)

    def peers(act, other):
        x = 1 - g if other else g
        act(x, lax.rem(chan + CH // 2, CH))

        def one(k, _):
            act(x, lax.rem(chan + CH // 2 - k, CH))
            act(x, lax.rem(chan + CH // 2 + k, CH))
            return 0

        lax.fori_loop(1, CH // 2, one, 0)
        if other:
            act(x, chan)

    small = [
        pltpu.make_async_copy(source, target, small_sem.at[n])
        for n, (source, target) in enumerate(
            [
                (order_hbm, order), (taps_hbm, taps), (twiddle_hbm, twiddle), (dft_hbm, dft),
                (slots_hbm, slots), (shuffle_hbm, shuffle), (turn_hbm, turn),
            ]
        )
    ]
    large = [
        [
            pltpu.make_async_copy(volts_hbm.at[p, a], volts.at[a, p], volts_sem.at[a, p])
            for p in range(2)
        ]
        for a in range(2)
    ]
    small[0].start()
    for copy in large[0] + small[1:4] + large[1] + small[4:]:
        copy.start()

    barrier = pltpu.get_barrier_semaphore()

    def greet(x, c):
        pl.semaphore_signal(barrier, inc=1, device_id=(c, x * Z + z), device_id_type=MESH)

    def greet_column(k, _):
        there = lax.rem(z + k, Z)
        for x in range(2):
            pl.semaphore_signal(
                barrier, inc=1, device_id=(chan, x * Z + there), device_id_type=MESH
            )
        return 0

    peers(greet, 0)
    peers(greet, 1)
    lax.fori_loop(1, Z, greet_column, 0)

    small[0].wait()
    spread = lax.broadcasted_iota(jnp.int32, (CH, 512), 1) % CH
    spread = spread == lax.broadcasted_iota(jnp.int32, (CH, 512), 0)
    rows = jnp.broadcast_to(order[...], (8, CH)).astype(F32).astype(BF16)
    goal = jnp.dot(rows, spread.astype(F32).astype(BF16), preferred_element_type=F32)[0:1]
    row = lax.broadcasted_iota(jnp.int32, (512, 512), 0)
    col = lax.broadcasted_iota(jnp.int32, (512, 512), 1)
    same = (row // N1 == goal.astype(jnp.int32)) & (row % N1 == col // CH)
    mover[...] = same.astype(F32).astype(BF16)

    def transform(s, a):
        for h in range(2):
            rows = pl.ds(h * 16, 16)

            def point(p, j):
                total = None
                for t in range(TAPS):
                    at = (s + t) * FINE + j * N2
                    term = taps[t : t + 1, j * N2 : (j + 1) * N2] * volts[
                        a, p, rows, at : at + N2
                    ].astype(F32)
                    total = term if total is None else total + term
                return total.astype(BF16).astype(F32)

            x = [(point(0, j), point(1, j)) for j in range(N1)]
            for f, (re, im) in enumerate(dft16(x)):
                c, d = twiddle[0, f : f + 1], twiddle[1, f : f + 1]
                at = pl.ds(f * CH + h * 16, 16)
                section[a, at, 0:N2] = (re * c + im * d).astype(BF16)
                section[a, at, N2 : 2 * N2] = (im * c - re * d).astype(BF16)
        moved = jnp.dot(mover[...], section[a], preferred_element_type=F32).astype(BF16)
        result = jnp.dot(moved, dft[...], preferred_element_type=F32)
        return result.reshape(CH, 2, HALF, 256)

    def spectrum(s):
        if s == 0:
            for copy in small[1:4] + large[0]:
                copy.wait()
        first[...] = transform(s, 0)
        if s == 0:
            for copy in large[1]:
                copy.wait()
        second = transform(s, 1)
        for h in range(2):
            both = jnp.concatenate([first[:, h], second[:, h]], axis=1).astype(BF16)
            for k in range(2):
                sent[2 * s + h, k * CH : (k + 1) * CH] = both[:, :, k * 128 : (k + 1) * 128]

    def keep(q):
        return pltpu.make_async_copy(sent.at[q, me], arrived.at[q, me], own_sem.at[q])

    def send(q, other):
        def one(x, c):
            pltpu.make_async_remote_copy(
                src_ref=sent.at[q, x * CH + c],
                dst_ref=arrived.at[q, me],
                send_sem=turn_send.at[q],
                recv_sem=turn_recv.at[q, other],
                device_id=(c, x * Z + z),
                device_id_type=MESH,
            ).start()

        peers(one, other)

    def columns():
        for copy in small[4:]:
            copy.wait()
        value = jnp.broadcast_to(slots[...], (8, 512))
        spread = lax.broadcasted_iota(jnp.int32, (512, 1024), 1) // 2
        spread = spread == lax.broadcasted_iota(jnp.int32, (512, 1024), 0)
        spread = spread.astype(F32).astype(BF16)
        high = jnp.dot((value // 32).astype(F32).astype(BF16), spread, preferred_element_type=F32)
        low = jnp.dot((value % 32).astype(F32).astype(BF16), spread, preferred_element_type=F32)
        station = (high * 32.0 + low)[0:1].astype(jnp.int32)
        source = 2 * station + lax.broadcasted_iota(jnp.int32, (1, 1024), 1) % 2

        def one_hot(e, _):
            row = lax.broadcasted_iota(jnp.int32, (128, 1), 0)
            row = (row // 64) * (64 * Z) + row % 64 + along(-e) * 64
            places[e] = (source == row).astype(F32).astype(BF16)
            return 0

        lax.fori_loop(0, 8, one_hot, 0)

    flying = []

    def forward(d, n, at):
        return pltpu.make_async_remote_copy(
            src_ref=blocks.at[d, *at],
            dst_ref=blocks.at[d + 1, *at],
            send_sem=ring_send.at[d, n],
            recv_sem=ring_recv.at[d, n],
            device_id=(chan, g * Z + along(1)),
            device_id_type=MESH,
        )

    def launch(copy):
        if len(flying) == DEPTH:
            flying.pop(0).wait_send()
        copy.start()
        flying.append(copy)

    def pass_on(d, q, n):
        if q == 0:
            at = (pl.ds(0, DEEP), pl.ds(pl.multiple_of(64 * (1 - g if n else g), 64), 64))
        else:
            at = (pl.ds(q * DEEP + n * (DEEP // PIECES), DEEP // PIECES),)
        return forward(d, q * PIECES + n, at)

    def first_of_half(q, there):
        return q * DEEP + lax.div(there, FAR) * (DEEP // 2)

    def pass_half(q, there):
        at = (pl.ds(first_of_half(q, there), DEEP // 2),)
        return forward(FAR - 1, q * PIECES, at)

    def multiply(d, start, count):
        value = None
        for k in range(count):
            term = lax.dot_general(
                left[start + k],
                blocks[d, start + k],
                (((1,), (1,)), ((), ())),
                preferred_element_type=F32,
            )
            value = term if value is None else value + term
        total[d] += value

    def gather(q, other):
        x = 1 - g if other else g
        if not other:
            keep(q).wait()
        several = arrived.at[q, pl.ds(0, CH if other else CH - 1)]
        pltpu.make_async_copy(several, several, turn_recv.at[q, other]).wait()

        def arrange(n, _):
            n = 2 * x + n
            rows = arrived[q, pl.ds(n * 16, 16)].reshape(256, 128)
            rows = jnp.dot(shuffle[...], rows, preferred_element_type=F32)
            rows = rows.reshape(DEEP, 2, 32, 128)
            rows = jnp.concatenate([rows[:, 0], rows[:, 1]], axis=-1).astype(BF16)
            turned = jnp.dot(rows.reshape(DEEP * 32, 256), turn[...], preferred_element_type=F32)
            at = pl.ds(pl.multiple_of(n * 32, 32), 32)
            low = pl.ds(pl.multiple_of(n * 32 + 128, 32), 32)
            several = pl.ds(q * DEEP, DEEP)
            blocks[0, several, at, :] = rows
            left[several, at, :] = rows
            left[several, low, :] = turned.astype(BF16).reshape(DEEP, 32, 256)
            return 0

        lax.fori_loop(0, 2, arrange, 0)

    def take(q):
        for other in range(2):
            gather(q, other)
            if q == 0:
                launch(pass_on(0, q, other))
        if q > 0:
            for n in range(PIECES):
                launch(pass_on(0, q, n))
        multiply(0, q * DEEP, DEEP)

    def receive(d, q):
        if d == FAR:
            pass_half(q, z).wait_recv()
            multiply(d, first_of_half(q, z), DEEP // 2)
            return
        for n in range(PIECES):
            pass_on(d - 1, q, n).wait_recv()
            if d < FAR - 1:
                launch(pass_on(d, q, n))
            elif n == PIECES - 1:
                launch(pass_half(q, along(1)))
            if q > 0:
                multiply(d, q * DEEP + n * (DEEP // PIECES), DEEP // PIECES)
        if q == 0:
            multiply(d, 0, DEEP)

    def to_partner(d):
        return pltpu.make_async_remote_copy(
            src_ref=partner.at[d],
            dst_ref=final.at[d, g],
            send_sem=partner_send.at[d],
            recv_sem=final_recv.at[d, g],
            device_id=(chan, (1 - g) * Z + z),
            device_id_type=MESH,
        )

    def to_column(d, x):
        return pltpu.make_async_remote_copy(
            src_ref=mirror.at[d, x],
            dst_ref=final.at[REST if d == FAR else 8 - d, g],
            send_sem=mirror_send.at[d, x],
            recv_sem=final_recv.at[REST if d == FAR else 8 - d, g],
            device_id=(chan, x * Z + along(-d)),
            device_id_type=MESH,
        )

    def finish(d):
        for p in range(2):
            mine = pl.ds(pl.multiple_of(p * 128 + g * 64, 64), 64)
            other = pl.ds(pl.multiple_of(p * 128 + (1 - g) * 64, 64), 64)
            final[d, g, p] = total[d, mine, :].astype(BF16)
            partner[d, p] = total[d, other, :].astype(BF16)
        to_partner(d).start()
        if d > 0:
            re = total[d, 0:128, :].T
            im = -total[d, 128:256, :].T
            for x in range(2):
                mirror[d, x, 0] = re[x * 64 : (x + 1) * 64].astype(BF16)
                mirror[d, x, 1] = im[x * 64 : (x + 1) * 64].astype(BF16)
                to_column(d, x).start()

    def placed(e, n):
        columns = slice(n * 256, (n + 1) * 256)
        block = places[FAR if e == REST else e, :, columns]
        return jnp.dot(final[e].reshape(256, 128), block, preferred_element_type=F32)

    def arrives(e, x):
        there = final.at[e, x]
        pltpu.make_async_copy(there, there, final_recv.at[e, x]).wait()

    def product():
        for e in range(8):
            if e < FAR:
                arrives(e, 1 - g)
            if e > FAR + 1:
                arrives(e, 0)
                arrives(e, 1)
        for n in range(4):
            tile = placed(0, n)
            for e in range(1, 8):
                if e not in LATE:
                    tile += placed(e, n)
            sums[n] = tile

    total[...] = jnp.zeros_like(total)
    spectrum(0)
    pl.semaphore_wait(barrier, PLANE - 1 + 2 * (Z - 1))
    for q in (0, 1):
        keep(q).start()
    for q in (0, 1):
        for n in range(SENDS):
            send(q, n)
    spectrum(1)
    for q in (2, 3):
        keep(q).start()
    for what, *which in ORDER:
        if what == "send":
            send(*which)
        elif what == "take":
            take(*which)
            if which[0] == QUARTERS - 1:
                finish(0)
        elif what == "pass":
            receive(*which)
            if which[1] == QUARTERS - 1:
                finish(which[0])
        elif what == "columns":
            columns()
        else:
            product()
    for e in (FAR + 1, REST):
        arrives(e, 0)
        arrives(e, 1)
    arrives(FAR, 1 - g)
    for n in range(4):
        tile = (sums[n] + placed(FAR + 1, n) + placed(FAR, n) + placed(REST, n)) * SCALE
        out[0, :, :, :, n * 256 : (n + 1) * 256] = tile.reshape(2, 2, 64, 256)

    for q in range(QUARTERS):
        several = sent.at[q, pl.ds(0, PLANE - 1)]
        pltpu.make_async_copy(several, several, turn_send.at[q]).wait()

    for copy in flying:
        copy.wait_send()
    for d in range(FAR + 1):
        to_partner(d).wait_send()
        if d > 0:
            for x in range(2):
                to_column(d, x).wait_send()


def cross(*operands):
    dma = pltpu.SemaphoreType.DMA
    return pl.pallas_call(
        cross_kernel,
        out_shape=jax.ShapeDtypeStruct((1, 2, 2, 64, 1024), F32),
        in_specs=[pl.BlockSpec(memory_space=pl.ANY)] * 8,
        out_specs=pl.BlockSpec(memory_space=pltpu.VMEM),
        scratch_shapes=[
            pltpu.VMEM((2, 2, CH, 7 * FINE), BF16),
            pltpu.VMEM((TAPS, FINE), F32),
            pltpu.VMEM((1, CH), jnp.int32),
            pltpu.VMEM((1, 512), jnp.int32),
            pltpu.VMEM((2, N1, N2), F32),
            pltpu.VMEM((256, 256), BF16),
            pltpu.VMEM((256, 256), BF16),
            pltpu.VMEM((256, 256), BF16),
            pltpu.VMEM((2, 512, 256), BF16),
            pltpu.VMEM((512, 512), BF16),
            pltpu.VMEM((CH, 2, HALF, 256), F32),
            pltpu.VMEM((QUARTERS, PLANE, 16, 128), BF16),
            pltpu.VMEM((QUARTERS, PLANE, 16, 128), BF16),
            pltpu.VMEM((FAR + 1, QUARTERS * DEEP, 128, 256), BF16),
            pltpu.VMEM((QUARTERS * DEEP, 256, 256), BF16),
            pltpu.VMEM((FAR + 1, 256, 128), F32),
            pltpu.VMEM((8, 128, 1024), BF16),
            pltpu.VMEM((4, 256, 256), F32),
            pltpu.VMEM((9, 2, 2, 64, 128), BF16),
            pltpu.VMEM((FAR + 1, 2, 64, 128), BF16),
            pltpu.VMEM((FAR + 1, 2, 2, 64, 128), BF16),
            dma((2, 2)),
            dma((7,)),
            dma((QUARTERS,)),
            dma((QUARTERS,)),
            dma((QUARTERS, 2)),
            dma((FAR, QUARTERS * PIECES)),
            dma((FAR, QUARTERS * PIECES)),
            dma((9, 2)),
            dma((FAR + 1,)),
            dma((FAR + 1, 2)),
        ],
        compiler_params=pltpu.CompilerParams(
            collective_id=0, has_side_effects=True, vmem_limit_bytes=60 * 2**20
        ),
        name="cross",
    )(*operands)


def local(volts, pfb_taps, channel_order, station_slot):
    order, slots = channel_order.reshape(1, CH), station_slot.reshape(1, -1)
    return cross(volts, pfb_taps, order, slots, *tables())


def solution(mesh):
    in_specs = (P(None, ("inp", "chan"), None, None), P(), P(), P())
    out_specs = P("chan", None, None, "inp", None)
    return jax.shard_map(local, mesh=mesh, in_specs=in_specs, out_specs=out_specs, check_vma=False)
```

```python
import functools
import math

import jax
import jax.numpy as jnp
import numpy as np
from jax import lax
from jax.experimental import pallas as pl
from jax.experimental.pallas import tpu as pltpu
from jax.sharding import PartitionSpec as P

F32 = jnp.float32
BF16 = jnp.bfloat16
MESH = pl.DeviceIdType.MESH

TAPS = 6
FINE = 2048
N1 = 16
N2 = 128
CH = 32
Z = 8
PLANE = 2 * CH
HALF = 8
QUARTERS = 4
DEEP = 4
FAR = 4
DEPTH = 3
PIECES = 2
SCALE = 2.0**-22


def tables():
    j2 = np.arange(N2)
    f1 = np.arange(N1)
    angle = 2 * math.pi * (f1[:, None] * j2[None, :]) / FINE
    twiddle = np.stack([np.cos(angle), np.sin(angle)]).astype(np.float32)
    theta = 2 * math.pi * (j2[:, None] * j2[None, :] % N2) / N2
    cosine, sine = np.cos(theta), np.sin(theta)
    full = np.zeros((2, N2, 2, 2, 64))
    for g in range(2):
        part = slice(64 * g, 64 * g + 64)
        full[0, :, g, 0] = cosine[:, part]
        full[1, :, g, 0] = sine[:, part]
        full[0, :, g, 1] = -sine[:, part]
        full[1, :, g, 1] = cosine[:, part]
    dft = full.reshape(256, 256).astype(jnp.bfloat16)
    shuffle = np.zeros((256, 256))
    for slot in range(16):
        for a in range(2):
            for f in range(HALF):
                shuffle[f * 32 + slot * 2 + a, slot * 16 + a * 8 + f] = 1
    turn = np.zeros((256, 256))
    for s in range(2):
        for f in range(64):
            turn[s * 128 + 64 + f, s * 128 + f] = 1
            turn[s * 128 + f, s * 128 + 64 + f] = -1
    return twiddle, dft, shuffle.astype(jnp.bfloat16), turn.astype(jnp.bfloat16)


def dft4(v):
    (ar, ai), (br, bi), (cr, ci), (dr, di) = v
    pr, pi, mr, mi = ar + cr, ai + ci, ar - cr, ai - ci
    qr, qi, nr, ni = br + dr, bi + di, br - dr, bi - di
    return [
        (pr + qr, pi + qi),
        (mr + ni, mi - nr),
        (pr - qr, pi - qi),
        (mr - ni, mi + nr),
    ]


def rotate(v, k):
    k = k % 16
    re, im = v
    if k == 0:
        return v
    if k == 4:
        return im, -re
    c, s = math.cos(2 * math.pi * k / 16), math.sin(2 * math.pi * k / 16)
    if k == 2:
        return (re + im) * c, (im - re) * c
    if k == 6:
        return (im - re) * s, (re + im) * -s
    return re * c + im * s, im * c - re * s


def dft16(x):
    inner = [dft4([x[4 * n + m] for n in range(4)]) for m in range(4)]
    out = [None] * 16
    for k in range(4):
        column = dft4([rotate(inner[m][k], m * k) for m in range(4)])
        for q in range(4):
            out[k + 4 * q] = column[q]
    return out


SENDS = 2
LATE = (FAR - 1, FAR, FAR + 1)
REST = 8
ORDER = (
    [("send", q, n) for q in (2, 3) for n in range(SENDS)]
    + [("columns",), ("take", 0), ("pass", 1, 0), ("take", 1), ("pass", 2, 0), ("pass", 1, 1)]
    + [("take", 2), ("pass", 2, 1), ("take", 3), ("pass", 1, 2), ("pass", 3, 0), ("pass", 1, 3)]
    + [("pass", 3, 1), ("pass", 2, 2), ("pass", 2, 3), ("pass", 3, 2), ("pass", 3, 3)]
    + [("pass", 4, 0), ("pass", 4, 1), ("product",), ("pass", 4, 2), ("pass", 4, 3)]
)


def cross_kernel(
    volts_hbm, taps_hbm, order_hbm, slots_hbm, twiddle_hbm, dft_hbm, shuffle_hbm, turn_hbm, out,
    volts, taps, order, slots, twiddle, dft, shuffle, turn,
    section, mover, first, sent, arrived, blocks, left, total, places, sums, final, partner, mirror,
    volts_sem, small_sem, own_sem, turn_send, turn_recv, ring_send, ring_recv,
    final_recv, partner_send, mirror_send,
):
    chan = lax.axis_index("chan")
    inp = lax.axis_index("inp")
    g = lax.div(inp, Z)
    z = lax.rem(inp, Z)
    me = g * CH + chan
    way = 1 - 2 * lax.rem(chan, 2)

    def along(hops):
        return lax.rem(z + hops * way + Z, Z)

    def peers(act, other):
        x = 1 - g if other else g
        act(x, lax.rem(chan + CH // 2, CH))

        def one(k, _):
            act(x, lax.rem(chan + CH // 2 - k, CH))
            act(x, lax.rem(chan + CH // 2 + k, CH))
            return 0

        lax.fori_loop(1, CH // 2, one, 0)
        if other:
            act(x, chan)

    small = [
        pltpu.make_async_copy(source, target, small_sem.at[n])
        for n, (source, target) in enumerate(
            [
                (order_hbm, order), (taps_hbm, taps), (twiddle_hbm, twiddle), (dft_hbm, dft),
                (slots_hbm, slots), (shuffle_hbm, shuffle), (turn_hbm, turn),
            ]
        )
    ]
    large = [
        [
            pltpu.make_async_copy(volts_hbm.at[p, a], volts.at[a, p], volts_sem.at[a, p])
            for p in range(2)
        ]
        for a in range(2)
    ]
    small[0].start()
    for copy in large[0] + small[1:4] + large[1] + small[4:]:
        copy.start()

    barrier = pltpu.get_barrier_semaphore()

    def greet(x, c):
        pl.semaphore_signal(barrier, inc=1, device_id=(c, x * Z + z), device_id_type=MESH)

    def greet_column(k, _):
        there = lax.rem(z + k, Z)
        for x in range(2):
            pl.semaphore_signal(
                barrier, inc=1, device_id=(chan, x * Z + there), device_id_type=MESH
            )
        return 0

    peers(greet, 0)
    peers(greet, 1)
    lax.fori_loop(1, Z, greet_column, 0)

    small[0].wait()
    spread = lax.broadcasted_iota(jnp.int32, (CH, 512), 1) % CH
    spread = spread == lax.broadcasted_iota(jnp.int32, (CH, 512), 0)
    rows = jnp.broadcast_to(order[...], (8, CH)).astype(F32).astype(BF16)
    goal = jnp.dot(rows, spread.astype(F32).astype(BF16), preferred_element_type=F32)[0:1]
    row = lax.broadcasted_iota(jnp.int32, (512, 512), 0)
    col = lax.broadcasted_iota(jnp.int32, (512, 512), 1)
    same = (row // N1 == goal.astype(jnp.int32)) & (row % N1 == col // CH)
    mover[...] = same.astype(F32).astype(BF16)

    def transform(s, a):
        for h in range(2):
            rows = pl.ds(h * 16, 16)

            def point(p, j):
                total = None
                for t in range(TAPS):
                    at = (s + t) * FINE + j * N2
                    term = taps[t : t + 1, j * N2 : (j + 1) * N2] * volts[
                        a, p, rows, at : at + N2
                    ].astype(F32)
                    total = term if total is None else total + term
                return total.astype(BF16).astype(F32)

            x = [(point(0, j), point(1, j)) for j in range(N1)]
            for f, (re, im) in enumerate(dft16(x)):
                c, d = twiddle[0, f : f + 1], twiddle[1, f : f + 1]
                at = pl.ds(f * CH + h * 16, 16)
                section[a, at, 0:N2] = (re * c + im * d).astype(BF16)
                section[a, at, N2 : 2 * N2] = (im * c - re * d).astype(BF16)
        moved = jnp.dot(mover[...], section[a], preferred_element_type=F32).astype(BF16)
        result = jnp.dot(moved, dft[...], preferred_element_type=F32)
        return result.reshape(CH, 2, HALF, 256)

    def spectrum(s):
        if s == 0:
            for copy in small[1:4] + large[0]:
                copy.wait()
        first[...] = transform(s, 0)
        if s == 0:
            for copy in large[1]:
                copy.wait()
        second = transform(s, 1)
        for h in range(2):
            both = jnp.concatenate([first[:, h], second[:, h]], axis=1).astype(BF16)
            for k in range(2):
                sent[2 * s + h, k * CH : (k + 1) * CH] = both[:, :, k * 128 : (k + 1) * 128]

    def keep(q):
        return pltpu.make_async_copy(sent.at[q, me], arrived.at[q, me], own_sem.at[q])

    def send(q, other):
        def one(x, c):
            pltpu.make_async_remote_copy(
                src_ref=sent.at[q, x * CH + c],
                dst_ref=arrived.at[q, me],
                send_sem=turn_send.at[q],
                recv_sem=turn_recv.at[q, other],
                device_id=(c, x * Z + z),
                device_id_type=MESH,
            ).start()

        peers(one, other)

    def columns():
        for copy in small[4:]:
            copy.wait()
        value = jnp.broadcast_to(slots[...], (8, 512))
        spread = lax.broadcasted_iota(jnp.int32, (512, 1024), 1) // 2
        spread = spread == lax.broadcasted_iota(jnp.int32, (512, 1024), 0)
        spread = spread.astype(F32).astype(BF16)
        high = jnp.dot((value // 32).astype(F32).astype(BF16), spread, preferred_element_type=F32)
        low = jnp.dot((value % 32).astype(F32).astype(BF16), spread, preferred_element_type=F32)
        station = (high * 32.0 + low)[0:1].astype(jnp.int32)
        source = 2 * station + lax.broadcasted_iota(jnp.int32, (1, 1024), 1) % 2

        def one_hot(e, _):
            row = lax.broadcasted_iota(jnp.int32, (128, 1), 0)
            row = (row // 64) * (64 * Z) + row % 64 + along(-e) * 64
            places[e] = (source == row).astype(F32).astype(BF16)
            return 0

        lax.fori_loop(0, 8, one_hot, 0)

    flying = []

    def forward(d, n, at):
        return pltpu.make_async_remote_copy(
            src_ref=blocks.at[d, *at],
            dst_ref=blocks.at[d + 1, *at],
            send_sem=ring_send.at[d, n],
            recv_sem=ring_recv.at[d, n],
            device_id=(chan, g * Z + along(1)),
            device_id_type=MESH,
        )

    def launch(copy):
        if len(flying) == DEPTH:
            flying.pop(0).wait_send()
        copy.start()
        flying.append(copy)

    def turned_round(d, n):
        return lax.rem(n + lax.div(along(FAR - d), FAR), PIECES)

    def pass_on(d, q, n, came):
        if q == 0 and d < FAR - 2:
            at = (pl.ds(0, DEEP), pl.ds(pl.multiple_of(64 * (1 - g if n else g), 64), 64))
        else:
            n = turned_round(came, n)
            at = (pl.ds(q * DEEP + n * (DEEP // PIECES), DEEP // PIECES),)
        return forward(d, q * PIECES + n, at)

    def first_of_half(q, there):
        return q * DEEP + lax.div(there, FAR) * (DEEP // 2)

    def pass_half(q, there):
        at = (pl.ds(first_of_half(q, there), DEEP // 2),)
        return forward(FAR - 1, q * PIECES, at)

    def multiply(d, start, count):
        value = None
        for k in range(count):
            term = lax.dot_general(
                left[start + k],
                blocks[d, start + k],
                (((1,), (1,)), ((), ())),
                preferred_element_type=F32,
            )
            value = term if value is None else value + term
        total[d] += value

    def gather(q, other):
        x = 1 - g if other else g
        if not other:
            keep(q).wait()
        several = arrived.at[q, pl.ds(0, CH if other else CH - 1)]
        pltpu.make_async_copy(several, several, turn_recv.at[q, other]).wait()

        def arrange(n, _):
            n = 2 * x + n
            rows = arrived[q, pl.ds(n * 16, 16)].reshape(256, 128)
            rows = jnp.dot(shuffle[...], rows, preferred_element_type=F32)
            rows = rows.reshape(DEEP, 2, 32, 128)
            rows = jnp.concatenate([rows[:, 0], rows[:, 1]], axis=-1).astype(BF16)
            turned = jnp.dot(rows.reshape(DEEP * 32, 256), turn[...], preferred_element_type=F32)
            at = pl.ds(pl.multiple_of(n * 32, 32), 32)
            low = pl.ds(pl.multiple_of(n * 32 + 128, 32), 32)
            several = pl.ds(q * DEEP, DEEP)
            blocks[0, several, at, :] = rows
            left[several, at, :] = rows
            left[several, low, :] = turned.astype(BF16).reshape(DEEP, 32, 256)
            return 0

        lax.fori_loop(0, 2, arrange, 0)

    def take(q):
        for other in range(2):
            gather(q, other)
            if q == 0:
                launch(pass_on(0, q, other, 0))
        if q > 0:
            for n in range(PIECES):
                launch(pass_on(0, q, n, 0))
        multiply(0, q * DEEP, DEEP)

    def receive(d, q):
        if d == FAR:
            pass_half(q, z).wait_recv()
            multiply(d, first_of_half(q, z), DEEP // 2)
            return
        for n in range(PIECES):
            pass_on(d - 1, q, n, d).wait_recv()
            if d == FAR - 1:
                if n == 0:
                    launch(pass_half(q, along(1)))
            elif q > 0 or d < FAR - 2:
                launch(pass_on(d, q, n, d))
            if q > 0:
                first_of_piece = q * DEEP + turned_round(d, n) * (DEEP // PIECES)
                multiply(d, first_of_piece, DEEP // PIECES)
        if q == 0:
            if d == FAR - 2:
                for n in range(PIECES):
                    launch(pass_on(d, q, n, d))
            multiply(d, 0, DEEP)

    def to_partner(d):
        return pltpu.make_async_remote_copy(
            src_ref=partner.at[d],
            dst_ref=final.at[d, g],
            send_sem=partner_send.at[d],
            recv_sem=final_recv.at[d, g],
            device_id=(chan, (1 - g) * Z + z),
            device_id_type=MESH,
        )

    def to_column(d, x):
        return pltpu.make_async_remote_copy(
            src_ref=mirror.at[d, x],
            dst_ref=final.at[REST if d == FAR else 8 - d, g],
            send_sem=mirror_send.at[d, x],
            recv_sem=final_recv.at[REST if d == FAR else 8 - d, g],
            device_id=(chan, x * Z + along(-d)),
            device_id_type=MESH,
        )

    def finish(d):
        if d > 0:
            re = total[d, 0:128, :].T
            im = -total[d, 128:256, :].T
            for x in range(2):
                mirror[d, x, 0] = re[x * 64 : (x + 1) * 64].astype(BF16)
                mirror[d, x, 1] = im[x * 64 : (x + 1) * 64].astype(BF16)
                to_column(d, x).start()
        for p in range(2):
            mine = pl.ds(pl.multiple_of(p * 128 + g * 64, 64), 64)
            other = pl.ds(pl.multiple_of(p * 128 + (1 - g) * 64, 64), 64)
            final[d, g, p] = total[d, mine, :].astype(BF16)
            partner[d, p] = total[d, other, :].astype(BF16)
        to_partner(d).start()

    def placed(e, n):
        columns = slice(n * 256, (n + 1) * 256)
        block = places[FAR if e == REST else e, :, columns]
        return jnp.dot(final[e].reshape(256, 128), block, preferred_element_type=F32)

    def arrives(e, x):
        there = final.at[e, x]
        pltpu.make_async_copy(there, there, final_recv.at[e, x]).wait()

    def product():
        for e in range(8):
            if e < FAR - 1:
                arrives(e, 1 - g)
            if e > FAR + 1:
                arrives(e, 0)
                arrives(e, 1)
        for n in range(4):
            tile = placed(0, n)
            for e in range(1, 8):
                if e not in LATE:
                    tile += placed(e, n)
            sums[n] = tile

    total[...] = jnp.zeros_like(total)
    spectrum(0)
    pl.semaphore_wait(barrier, PLANE - 1 + 2 * (Z - 1))
    for q in (0, 1):
        keep(q).start()
    for q in (0, 1):
        for n in range(SENDS):
            send(q, n)
    spectrum(1)
    for q in (2, 3):
        keep(q).start()
    for what, *which in ORDER:
        if what == "send":
            send(*which)
        elif what == "take":
            take(*which)
            if which[0] == QUARTERS - 1:
                finish(0)
        elif what == "pass":
            receive(*which)
            if which[1] == QUARTERS - 1:
                finish(which[0])
        elif what == "columns":
            columns()
        else:
            product()
    arrives(FAR - 1, 1 - g)
    arrives(FAR + 1, 0)
    arrives(FAR + 1, 1)
    arrives(FAR, 1 - g)
    for n in range(4):
        sums[n] += placed(FAR - 1, n) + placed(FAR + 1, n) + placed(FAR, n)
    arrives(REST, 0)
    arrives(REST, 1)
    for n in range(4):
        tile = sums[n] + placed(REST, n)
        out[0, :, :, :, n * 256 : (n + 1) * 256] = tile.astype(BF16).reshape(2, 2, 64, 256)

    for q in range(QUARTERS):
        several = sent.at[q, pl.ds(0, PLANE - 1)]
        pltpu.make_async_copy(several, several, turn_send.at[q]).wait()

    for copy in flying:
        copy.wait_send()
    for d in range(FAR + 1):
        to_partner(d).wait_send()
        if d > 0:
            for x in range(2):
                to_column(d, x).wait_send()


def cross(*operands):
    dma = pltpu.SemaphoreType.DMA
    return pl.pallas_call(
        cross_kernel,
        out_shape=jax.ShapeDtypeStruct((1, 2, 2, 64, 1024), BF16),
        in_specs=[pl.BlockSpec(memory_space=pl.ANY)] * 8,
        out_specs=pl.BlockSpec(memory_space=pltpu.VMEM),
        scratch_shapes=[
            pltpu.VMEM((2, 2, CH, 7 * FINE), BF16),
            pltpu.VMEM((TAPS, FINE), F32),
            pltpu.VMEM((1, CH), jnp.int32),
            pltpu.VMEM((1, 512), jnp.int32),
            pltpu.VMEM((2, N1, N2), F32),
            pltpu.VMEM((256, 256), BF16),
            pltpu.VMEM((256, 256), BF16),
            pltpu.VMEM((256, 256), BF16),
            pltpu.VMEM((2, 512, 256), BF16),
            pltpu.VMEM((512, 512), BF16),
            pltpu.VMEM((CH, 2, HALF, 256), F32),
            pltpu.VMEM((QUARTERS, PLANE, 16, 128), BF16),
            pltpu.VMEM((QUARTERS, PLANE, 16, 128), BF16),
            pltpu.VMEM((FAR + 1, QUARTERS * DEEP, 128, 256), BF16),
            pltpu.VMEM((QUARTERS * DEEP, 256, 256), BF16),
            pltpu.VMEM((FAR + 1, 256, 128), F32),
            pltpu.VMEM((8, 128, 1024), BF16),
            pltpu.VMEM((4, 256, 256), F32),
            pltpu.VMEM((9, 2, 2, 64, 128), BF16),
            pltpu.VMEM((FAR + 1, 2, 64, 128), BF16),
            pltpu.VMEM((FAR + 1, 2, 2, 64, 128), BF16),
            dma((2, 2)),
            dma((7,)),
            dma((QUARTERS,)),
            dma((QUARTERS,)),
            dma((QUARTERS, 2)),
            dma((FAR, QUARTERS * PIECES)),
            dma((FAR, QUARTERS * PIECES)),
            dma((9, 2)),
            dma((FAR + 1,)),
            dma((FAR + 1, 2)),
        ],
        compiler_params=pltpu.CompilerParams(
            collective_id=0, has_side_effects=True, vmem_limit_bytes=60 * 2**20
        ),
        name="cross",
    )(*operands)


def local(volts, pfb_taps, channel_order, station_slot):
    order, slots = channel_order.reshape(1, CH), station_slot.reshape(1, -1)
    return cross(volts, pfb_taps, order, slots, *tables()).astype(F32) * SCALE


def solution(mesh):
    in_specs = (P(None, ("inp", "chan"), None, None), P(), P(), P())
    out_specs = P("chan", None, None, "inp", None)
    return jax.shard_map(local, mesh=mesh, in_specs=in_specs, out_specs=out_specs, check_vma=False)
```

```python
import functools
import math

import jax
import jax.numpy as jnp
import numpy as np
from jax import lax
from jax.experimental import pallas as pl
from jax.experimental.pallas import tpu as pltpu
from jax.sharding import PartitionSpec as P

F32 = jnp.float32
BF16 = jnp.bfloat16
MESH = pl.DeviceIdType.MESH

TAPS = 6
FINE = 2048
N1 = 16
N2 = 128
CH = 32
Z = 8
PLANE = 2 * CH
HALF = 8
QUARTERS = 4
DEEP = 4
FAR = 4
DEPTH = 3
PIECES = 2
SCALE = 2.0**-22


def tables():
    j2 = np.arange(N2)
    f1 = np.arange(N1)
    angle = 2 * math.pi * (f1[:, None] * j2[None, :]) / FINE
    twiddle = np.stack([np.cos(angle), np.sin(angle)]).astype(np.float32)
    theta = 2 * math.pi * (j2[:, None] * j2[None, :] % N2) / N2
    cosine, sine = np.cos(theta), np.sin(theta)
    full = np.zeros((2, N2, 2, 2, 64))
    for g in range(2):
        part = slice(64 * g, 64 * g + 64)
        full[0, :, g, 0] = cosine[:, part]
        full[1, :, g, 0] = sine[:, part]
        full[0, :, g, 1] = -sine[:, part]
        full[1, :, g, 1] = cosine[:, part]
    dft = full.reshape(256, 256).astype(jnp.bfloat16)
    shuffle = np.zeros((256, 256))
    for slot in range(16):
        for a in range(2):
            for f in range(HALF):
                shuffle[f * 32 + slot * 2 + a, slot * 16 + a * 8 + f] = 1
    turn = np.zeros((256, 256))
    for s in range(2):
        for f in range(64):
            turn[s * 128 + 64 + f, s * 128 + f] = 1
            turn[s * 128 + f, s * 128 + 64 + f] = -1
    return twiddle, dft, shuffle.astype(jnp.bfloat16), turn.astype(jnp.bfloat16)


def dft4(v):
    (ar, ai), (br, bi), (cr, ci), (dr, di) = v
    pr, pi, mr, mi = ar + cr, ai + ci, ar - cr, ai - ci
    qr, qi, nr, ni = br + dr, bi + di, br - dr, bi - di
    return [
        (pr + qr, pi + qi),
        (mr + ni, mi - nr),
        (pr - qr, pi - qi),
        (mr - ni, mi + nr),
    ]


def rotate(v, k):
    k = k % 16
    re, im = v
    if k == 0:
        return v
    if k == 4:
        return im, -re
    c, s = math.cos(2 * math.pi * k / 16), math.sin(2 * math.pi * k / 16)
    if k == 2:
        return (re + im) * c, (im - re) * c
    if k == 6:
        return (im - re) * s, (re + im) * -s
    return re * c + im * s, im * c - re * s


def dft16(x):
    inner = [dft4([x[4 * n + m] for n in range(4)]) for m in range(4)]
    out = [None] * 16
    for k in range(4):
        column = dft4([rotate(inner[m][k], m * k) for m in range(4)])
        for q in range(4):
            out[k + 4 * q] = column[q]
    return out


SENDS = 2
LATE = (FAR - 1, FAR, FAR + 1, FAR + 2)
REST = 8
ORDER = (
    [("send", q, n) for q in (2, 3) for n in range(SENDS)]
    + [("columns",), ("take", 0), ("pass", 1, 0), ("take", 1), ("pass", 2, 0), ("pass", 1, 1)]
    + [("take", 2), ("pass", 2, 1), ("take", 3), ("pass", 1, 2), ("pass", 3, 0), ("pass", 1, 3)]
    + [("pass", 3, 1), ("pass", 2, 2), ("pass", 2, 3), ("pass", 3, 2), ("pass", 3, 3)]
    + [("pass", 4, 0), ("pass", 4, 1), ("product",), ("pass", 4, 2), ("pass", 4, 3)]
)


def cross_kernel(
    volts_hbm, taps_hbm, order_hbm, slots_hbm, twiddle_hbm, dft_hbm, shuffle_hbm, turn_hbm, out,
    volts, taps, order, slots, twiddle, dft, shuffle, turn,
    section, mover, first, sent, arrived, blocks, left, total, places, sums, final, partner, mirror,
    volts_sem, small_sem, own_sem, turn_send, turn_recv, ring_send, ring_recv,
    final_recv, partner_send, mirror_send,
):
    chan = lax.axis_index("chan")
    inp = lax.axis_index("inp")
    g = lax.div(inp, Z)
    z = lax.rem(inp, Z)
    me = g * CH + chan
    way = 1 - 2 * lax.rem(chan, 2)

    def along(hops):
        return lax.rem(z + hops * way + Z, Z)

    def peers(act, other):
        x = 1 - g if other else g
        act(x, lax.rem(chan + CH // 2, CH))

        def one(k, _):
            act(x, lax.rem(chan + CH // 2 - k, CH))
            act(x, lax.rem(chan + CH // 2 + k, CH))
            return 0

        lax.fori_loop(1, CH // 2, one, 0)
        if other:
            act(x, chan)

    small = [
        pltpu.make_async_copy(source, target, small_sem.at[n])
        for n, (source, target) in enumerate(
            [
                (order_hbm, order), (taps_hbm, taps), (twiddle_hbm, twiddle), (dft_hbm, dft),
                (slots_hbm, slots), (shuffle_hbm, shuffle), (turn_hbm, turn),
            ]
        )
    ]
    large = [
        [
            pltpu.make_async_copy(volts_hbm.at[p, a], volts.at[a, p], volts_sem.at[a, p])
            for p in range(2)
        ]
        for a in range(2)
    ]
    small[0].start()
    for copy in large[0] + small[1:4] + large[1] + small[4:]:
        copy.start()

    barrier = pltpu.get_barrier_semaphore()

    def greet(x, c):
        pl.semaphore_signal(barrier, inc=1, device_id=(c, x * Z + z), device_id_type=MESH)

    def greet_column(k, _):
        there = lax.rem(z + k, Z)
        for x in range(2):
            pl.semaphore_signal(
                barrier, inc=1, device_id=(chan, x * Z + there), device_id_type=MESH
            )
        return 0

    peers(greet, 0)
    peers(greet, 1)
    lax.fori_loop(1, Z, greet_column, 0)

    small[0].wait()
    spread = lax.broadcasted_iota(jnp.int32, (CH, 512), 1) % CH
    spread = spread == lax.broadcasted_iota(jnp.int32, (CH, 512), 0)
    rows = jnp.broadcast_to(order[...], (8, CH)).astype(F32).astype(BF16)
    goal = jnp.dot(rows, spread.astype(F32).astype(BF16), preferred_element_type=F32)[0:1]
    row = lax.broadcasted_iota(jnp.int32, (512, 512), 0)
    col = lax.broadcasted_iota(jnp.int32, (512, 512), 1)
    same = (row // N1 == goal.astype(jnp.int32)) & (row % N1 == col // CH)
    mover[...] = same.astype(F32).astype(BF16)

    def transform(s, a):
        for h in range(2):
            rows = pl.ds(h * 16, 16)

            def point(p, j):
                total = None
                for t in range(TAPS):
                    at = (s + t) * FINE + j * N2
                    term = taps[t : t + 1, j * N2 : (j + 1) * N2] * volts[
                        a, p, rows, at : at + N2
                    ].astype(F32)
                    total = term if total is None else total + term
                return total.astype(BF16).astype(F32)

            x = [(point(0, j), point(1, j)) for j in range(N1)]
            for f, (re, im) in enumerate(dft16(x)):
                c, d = twiddle[0, f : f + 1], twiddle[1, f : f + 1]
                at = pl.ds(f * CH + h * 16, 16)
                section[a, at, 0:N2] = (re * c + im * d).astype(BF16)
                section[a, at, N2 : 2 * N2] = (im * c - re * d).astype(BF16)
        moved = jnp.dot(mover[...], section[a], preferred_element_type=F32).astype(BF16)
        result = jnp.dot(moved, dft[...], preferred_element_type=F32)
        return result.reshape(CH, 2, HALF, 256)

    def spectrum(s):
        if s == 0:
            for copy in small[1:4] + large[0]:
                copy.wait()
        first[...] = transform(s, 0)
        if s == 0:
            for copy in large[1]:
                copy.wait()
        second = transform(s, 1)
        for h in range(2):
            both = jnp.concatenate([first[:, h], second[:, h]], axis=1).astype(BF16)
            for k in range(2):
                sent[2 * s + h, k * CH : (k + 1) * CH] = both[:, :, k * 128 : (k + 1) * 128]

    def keep(q):
        return pltpu.make_async_copy(sent.at[q, me], arrived.at[q, me], own_sem.at[q])

    def send(q, other):
        def one(x, c):
            pltpu.make_async_remote_copy(
                src_ref=sent.at[q, x * CH + c],
                dst_ref=arrived.at[q, me],
                send_sem=turn_send.at[q],
                recv_sem=turn_recv.at[q, other],
                device_id=(c, x * Z + z),
                device_id_type=MESH,
            ).start()

        peers(one, other)

    def columns():
        for copy in small[4:]:
            copy.wait()
        value = jnp.broadcast_to(slots[...], (8, 512))
        spread = lax.broadcasted_iota(jnp.int32, (512, 1024), 1) // 2
        spread = spread == lax.broadcasted_iota(jnp.int32, (512, 1024), 0)
        spread = spread.astype(F32).astype(BF16)
        high = jnp.dot((value // 32).astype(F32).astype(BF16), spread, preferred_element_type=F32)
        low = jnp.dot((value % 32).astype(F32).astype(BF16), spread, preferred_element_type=F32)
        station = (high * 32.0 + low)[0:1].astype(jnp.int32)
        source = 2 * station + lax.broadcasted_iota(jnp.int32, (1, 1024), 1) % 2

        def one_hot(e, _):
            row = lax.broadcasted_iota(jnp.int32, (128, 1), 0)
            row = (row // 64) * (64 * Z) + row % 64 + along(-e) * 64
            places[e] = (source == row).astype(F32).astype(BF16)
            return 0

        lax.fori_loop(0, 8, one_hot, 0)

    flying = []

    def forward(d, n, at):
        return pltpu.make_async_remote_copy(
            src_ref=blocks.at[d, *at],
            dst_ref=blocks.at[d + 1, *at],
            send_sem=ring_send.at[d, n],
            recv_sem=ring_recv.at[d, n],
            device_id=(chan, g * Z + along(1)),
            device_id_type=MESH,
        )

    def launch(copy):
        if len(flying) == DEPTH:
            flying.pop(0).wait_send()
        copy.start()
        flying.append(copy)

    def turned_round(d, n):
        return lax.rem(n + lax.div(along(FAR - d), FAR), PIECES)

    def pass_on(d, q, n, came):
        if q == 0 and d < FAR - 2:
            at = (pl.ds(0, DEEP), pl.ds(pl.multiple_of(64 * (1 - g if n else g), 64), 64))
        else:
            n = turned_round(came, n)
            at = (pl.ds(q * DEEP + n * (DEEP // PIECES), DEEP // PIECES),)
        return forward(d, q * PIECES + n, at)

    def first_of_half(q, there):
        return q * DEEP + lax.div(there, FAR) * (DEEP // 2)

    def pass_half(q, there):
        at = (pl.ds(first_of_half(q, there), DEEP // 2),)
        return forward(FAR - 1, q * PIECES, at)

    def multiply(d, start, count):
        value = None
        for k in range(count):
            term = lax.dot_general(
                left[start + k],
                blocks[d, start + k],
                (((1,), (1,)), ((), ())),
                preferred_element_type=F32,
            )
            value = term if value is None else value + term
        total[d] += value

    def gather(q, other):
        x = 1 - g if other else g
        if not other:
            keep(q).wait()
        several = arrived.at[q, pl.ds(0, CH if other else CH - 1)]
        pltpu.make_async_copy(several, several, turn_recv.at[q, other]).wait()

        def arrange(n, _):
            n = 2 * x + n
            rows = arrived[q, pl.ds(n * 16, 16)].reshape(256, 128)
            rows = jnp.dot(shuffle[...], rows, preferred_element_type=F32)
            rows = rows.reshape(DEEP, 2, 32, 128)
            rows = jnp.concatenate([rows[:, 0], rows[:, 1]], axis=-1).astype(BF16)
            turned = jnp.dot(rows.reshape(DEEP * 32, 256), turn[...], preferred_element_type=F32)
            at = pl.ds(pl.multiple_of(n * 32, 32), 32)
            low = pl.ds(pl.multiple_of(n * 32 + 128, 32), 32)
            several = pl.ds(q * DEEP, DEEP)
            blocks[0, several, at, :] = rows
            left[several, at, :] = rows
            left[several, low, :] = turned.astype(BF16).reshape(DEEP, 32, 256)
            return 0

        lax.fori_loop(0, 2, arrange, 0)

    def take(q):
        for other in range(2):
            gather(q, other)
            if q == 0:
                launch(pass_on(0, q, other, 0))
        if q > 0:
            for n in range(PIECES):
                launch(pass_on(0, q, n, 0))
        multiply(0, q * DEEP, DEEP)

    def receive(d, q):
        if d == FAR:
            pass_half(q, z).wait_recv()
            multiply(d, first_of_half(q, z), DEEP // 2)
            return
        for n in range(PIECES):
            pass_on(d - 1, q, n, d).wait_recv()
            if d == FAR - 1:
                if n == 0:
                    launch(pass_half(q, along(1)))
            elif q > 0 or d < FAR - 2:
                launch(pass_on(d, q, n, d))
            if q > 0:
                first_of_piece = q * DEEP + turned_round(d, n) * (DEEP // PIECES)
                multiply(d, first_of_piece, DEEP // PIECES)
        if q == 0:
            if d == FAR - 2:
                for n in range(PIECES):
                    launch(pass_on(d, q, n, d))
            multiply(d, 0, DEEP)

    def to_partner(d):
        return pltpu.make_async_remote_copy(
            src_ref=partner.at[d],
            dst_ref=final.at[d, g],
            send_sem=partner_send.at[d],
            recv_sem=final_recv.at[d, g],
            device_id=(chan, (1 - g) * Z + z),
            device_id_type=MESH,
        )

    def to_column(d, x):
        return pltpu.make_async_remote_copy(
            src_ref=mirror.at[d, x],
            dst_ref=final.at[REST if d == FAR else 8 - d, g],
            send_sem=mirror_send.at[d, x],
            recv_sem=final_recv.at[REST if d == FAR else 8 - d, g],
            device_id=(chan, x * Z + along(-d)),
            device_id_type=MESH,
        )

    def finish(d):
        if d > 0:
            re = total[d, 0:128, :].T
            im = -total[d, 128:256, :].T
            for x in range(2):
                mirror[d, x, 0] = re[x * 64 : (x + 1) * 64].astype(BF16)
                mirror[d, x, 1] = im[x * 64 : (x + 1) * 64].astype(BF16)
            to_column(d, 1 - g).start()
            to_column(d, g).start()
        for p in range(2):
            mine = pl.ds(pl.multiple_of(p * 128 + g * 64, 64), 64)
            other = pl.ds(pl.multiple_of(p * 128 + (1 - g) * 64, 64), 64)
            final[d, g, p] = total[d, mine, :].astype(BF16)
            partner[d, p] = total[d, other, :].astype(BF16)
        to_partner(d).start()

    def placed(e, n):
        columns = slice(n * 256, (n + 1) * 256)
        block = places[FAR if e == REST else e, :, columns]
        return jnp.dot(final[e].reshape(256, 128), block, preferred_element_type=F32)

    def arrives(e, x):
        there = final.at[e, x]
        pltpu.make_async_copy(there, there, final_recv.at[e, x]).wait()

    def product():
        for e in range(8):
            if e < FAR - 1:
                arrives(e, 1 - g)
            if e > FAR + 2:
                arrives(e, 0)
                arrives(e, 1)
        for n in range(4):
            tile = placed(0, n)
            for e in range(1, 8):
                if e not in LATE:
                    tile += placed(e, n)
            sums[n] = tile

    total[...] = jnp.zeros_like(total)
    spectrum(0)
    pl.semaphore_wait(barrier, PLANE - 1 + 2 * (Z - 1))
    for q in (0, 1):
        keep(q).start()
    for q in (0, 1):
        for n in range(SENDS):
            send(q, n)
    spectrum(1)
    for q in (2, 3):
        keep(q).start()
    for what, *which in ORDER:
        if what == "send":
            send(*which)
        elif what == "take":
            take(*which)
            if which[0] == QUARTERS - 1:
                finish(0)
        elif what == "pass":
            receive(*which)
            if which[1] == QUARTERS - 1:
                finish(which[0])
        elif what == "columns":
            columns()
        else:
            product()
    arrives(FAR - 1, 1 - g)
    for e in (FAR + 2, FAR + 1):
        arrives(e, 0)
        arrives(e, 1)
    arrives(FAR, 1 - g)
    for n in range(4):
        for e in LATE:
            sums[n] += placed(e, n)
    arrives(REST, 0)
    arrives(REST, 1)
    for n in range(4):
        tile = sums[n] + placed(REST, n)
        out[0, :, :, :, n * 256 : (n + 1) * 256] = tile.astype(BF16).reshape(2, 2, 64, 256)

    for q in range(QUARTERS):
        several = sent.at[q, pl.ds(0, PLANE - 1)]
        pltpu.make_async_copy(several, several, turn_send.at[q]).wait()

    for copy in flying:
        copy.wait_send()
    for d in range(FAR + 1):
        to_partner(d).wait_send()
        if d > 0:
            for x in range(2):
                to_column(d, x).wait_send()


def cross(*operands):
    dma = pltpu.SemaphoreType.DMA
    return pl.pallas_call(
        cross_kernel,
        out_shape=jax.ShapeDtypeStruct((1, 2, 2, 64, 1024), BF16),
        in_specs=[pl.BlockSpec(memory_space=pl.ANY)] * 8,
        out_specs=pl.BlockSpec(memory_space=pltpu.VMEM),
        scratch_shapes=[
            pltpu.VMEM((2, 2, CH, 7 * FINE), BF16),
            pltpu.VMEM((TAPS, FINE), F32),
            pltpu.VMEM((1, CH), jnp.int32),
            pltpu.VMEM((1, 512), jnp.int32),
            pltpu.VMEM((2, N1, N2), F32),
            pltpu.VMEM((256, 256), BF16),
            pltpu.VMEM((256, 256), BF16),
            pltpu.VMEM((256, 256), BF16),
            pltpu.VMEM((2, 512, 256), BF16),
            pltpu.VMEM((512, 512), BF16),
            pltpu.VMEM((CH, 2, HALF, 256), F32),
            pltpu.VMEM((QUARTERS, PLANE, 16, 128), BF16),
            pltpu.VMEM((QUARTERS, PLANE, 16, 128), BF16),
            pltpu.VMEM((FAR + 1, QUARTERS * DEEP, 128, 256), BF16),
            pltpu.VMEM((QUARTERS * DEEP, 256, 256), BF16),
            pltpu.VMEM((FAR + 1, 256, 128), F32),
            pltpu.VMEM((8, 128, 1024), BF16),
            pltpu.VMEM((4, 256, 256), F32),
            pltpu.VMEM((9, 2, 2, 64, 128), BF16),
            pltpu.VMEM((FAR + 1, 2, 64, 128), BF16),
            pltpu.VMEM((FAR + 1, 2, 2, 64, 128), BF16),
            dma((2, 2)),
            dma((7,)),
            dma((QUARTERS,)),
            dma((QUARTERS,)),
            dma((QUARTERS, 2)),
            dma((FAR, QUARTERS * PIECES)),
            dma((FAR, QUARTERS * PIECES)),
            dma((9, 2)),
            dma((FAR + 1,)),
            dma((FAR + 1, 2)),
        ],
        compiler_params=pltpu.CompilerParams(
            collective_id=0, has_side_effects=True, vmem_limit_bytes=60 * 2**20
        ),
        name="cross",
    )(*operands)


def local(volts, pfb_taps, channel_order, station_slot):
    order, slots = channel_order.reshape(1, CH), station_slot.reshape(1, -1)
    return cross(volts, pfb_taps, order, slots, *tables()).astype(F32) * SCALE


def solution(mesh):
    in_specs = (P(None, ("inp", "chan"), None, None), P(), P(), P())
    out_specs = P("chan", None, None, "inp", None)
    return jax.shard_map(local, mesh=mesh, in_specs=in_specs, out_specs=out_specs, check_vma=False)
```
